256 devices in a mesh: ctx: 64 (over x, z, core), tp: 4 (over y).
Axes of the slice: x: 4, y: 4, z: 8, core: 2. Of those that a mesh axis runs over, the one named last changes fastest.
Arguments:
- queries: bfloat16 [16384, 4096], P('ctx', 'tp'), may hold values from -6 to 6
- keys: bfloat16 [16384, 4096], P('ctx', 'tp'), may hold values from -6 to 6
- values: bfloat16 [16384, 4096], P('ctx', 'tp'), may hold values from -6 to 6
- gates: bfloat16 [16384, 4096], P('ctx', 'tp'), may hold values from -8 to 8
- cotangent: bfloat16 [16384, 4096], P('ctx', 'tp'), may hold values from -6 to 6
- doc_ids: int32 [16384], P('ctx'), may hold values from 0 to 31, never falling along the last dimension, each value on 1 to 1024 neighbouring positions
Outputs:
- query_grad: bfloat16 [16384, 4096], P('ctx', 'tp')
- key_grad: bfloat16 [16384, 4096], P('ctx', 'tp')
- value_grad: bfloat16 [16384, 4096], P('ctx', 'tp')
- gate_grad: bfloat16 [16384, 4096], P('ctx', 'tp')
The draws below stay inside these ranges and needn't reach their ends.
Inputs may be any that keep to these rules, and one draw needn't show every extreme that they name: doc_ids never fall along the sequence; each document holds 1 to 1024 positions, at least one exactly 1024.
All inputs are finite; a program needn't handle non-finite values.
Results may differ from the reference program's by a relative error of at most 0.0058.
Values may be sent and summed in bfloat16 or wider, within the bound.
No kernel may reach another device: no remote copies, remote signals or barrier semaphores. Data moves between devices by JAX's collectives and lax.ppermute only.
A program may use at most 192 MiB of HBM per device.

```python
import math
import jax
import jax.numpy as jnp
import numpy as np
from jax import lax

HEADS = 32
HEAD = 128
TOK_DEV = 256
TOKENS = 16384
N_CTX = 64


def steps_of(key, extent, split, least, largest):
    factor_of = 1.0
    for dim, blocks in split:
        steps = jax.random.uniform(jax.random.fold_in(jax.random.fold_in(key, 6), dim), (blocks,), jnp.float32, least / len(split), largest / len(split))
        factor_of = factor_of * jnp.repeat(jnp.exp(steps), extent[dim] // blocks).reshape((-1,) + (1,) * (len(extent) - 1 - dim))
    return factor_of


def profile(amount, total, limit, lean):
    loads = [(1 << 20) // math.isqrt(rank ** lean) + 1 for rank in range(2, amount + 1)]
    spare, counts = total - limit - (amount - 1), [1] * (amount - 1)
    while spare > 0:
        movable = [i for i in range(amount - 1) if counts[i] < limit]
        mass, budget = sum([loads[i] for i in movable]), spare
        for i in movable:
            extra = min(limit - counts[i], max(1, budget * loads[i] // mass), spare)
            counts[i] = counts[i] + extra
            spare = spare - extra
    return np.array([limit] + counts)


def uneven_parts(rng, count, total, most, slope):
    if count == 2:
        one = jax.random.randint(rng, (), max(1, total - most), min(most, total - 1) + 1)
        return jnp.stack([one, total - one])
    sizes = jnp.asarray(profile(count, total, most, slope), jnp.int32)
    couples = (count - 1) // 2
    donor, sink = sizes[1:1 + 2 * couples:2], sizes[2:2 + 2 * couples:2]
    margin = jnp.minimum(donor - 1, most - sink)
    passed = jax.random.randint(jax.random.fold_in(rng, 1), (couples,), 0, 1 << 20) % (margin + 1)
    sizes = sizes.at[1:1 + 2 * couples:2].set(donor - passed).at[2:2 + 2 * couples:2].set(sink + passed)
    return sizes[jax.random.permutation(jax.random.fold_in(rng, 2), count)]


def noise(stream_key, dims, width, most, split=(), kind=jnp.bfloat16):
    gain = steps_of(stream_key, dims, split, -0.22, 0.18) if split else 1.0
    array = jax.random.normal(stream_key, dims, jnp.float32) * width * gain
    return jnp.minimum(jnp.maximum(array, -most), most).astype(kind)


def setup_inputs(seed: int = 0) -> dict:
    streams_of = jax.random.split(jax.random.key(seed), 7)
    queries = noise(streams_of[0], (TOKENS, HEADS * HEAD), 1.0, 6.0, ((0, 64), (1, 4)))
    keys = noise(streams_of[1], (TOKENS, HEADS * HEAD), 1.0, 6.0, ((0, 64), (1, 4)))
    values = noise(streams_of[2], (TOKENS, HEADS * HEAD), 1.0, 6.0, ((0, 64), (1, 4)))
    gates = noise(streams_of[3], (TOKENS, HEADS * HEAD), 1.5, 8.0, ((0, 64), (1, 4)))
    cotangent = noise(streams_of[4], (TOKENS, HEADS * HEAD), 1.0, 6.0, ((0, 64), (1, 4)))
    doc_ids = jnp.searchsorted(jnp.cumsum(uneven_parts(streams_of[5], N_CTX // 2, TOKENS, 4 * TOK_DEV, 2)), jnp.arange(TOKENS), side="right").astype(jnp.int32)
    return dict(queries=queries, keys=keys, values=values, gates=gates, cotangent=cotangent, doc_ids=doc_ids)


EPSILON = 1e-06

def masked_scores(left_rows, right_rows, causal):
    raw_scores = jnp.einsum('thd,shd->hts', left_rows.astype(jnp.float32), right_rows.astype(jnp.float32))
    return jnp.where(causal[None], raw_scores, 0.0).astype(jnp.bfloat16)

def widen(state):
    narrow = lax.optimization_barrier(state.astype(jnp.bfloat16))
    return narrow.astype(jnp.float32)

def reference(queries, keys, values, gates, cotangent, doc_ids):
    block_shape = (N_CTX, TOK_DEV, HEADS, HEAD)
    feature_total = HEADS * HEAD
    query_blocks = queries.reshape(block_shape)
    key_blocks = keys.reshape(block_shape)
    value_blocks = values.reshape(block_shape)
    gate_blocks = gates.reshape(block_shape)
    grad_blocks = cotangent.reshape(block_shape)
    id_blocks = doc_ids.reshape(N_CTX, TOK_DEV)
    firsts = id_blocks[:, 0]
    lasts = id_blocks[:, TOK_DEV - 1]
    filler = jnp.full((1,), -1, jnp.int32)
    previous = jnp.concatenate([filler, lasts[:-1]])
    following = jnp.concatenate([firsts[1:], filler])
    ordinal = jnp.arange(N_CTX, dtype=jnp.int32)
    upward = ((ordinal[None, :] < ordinal[:, None]) & (lasts[None, :] == previous[:, None])).astype(jnp.float32)
    downward = ((ordinal[None, :] > ordinal[:, None]) & (firsts[None, :] == following[:, None])).astype(jnp.float32)
    positions = jnp.arange(TOK_DEV, dtype=jnp.int32)

    def causal_of(block_ids):
        return (positions[None, :] <= positions[:, None]) & (block_ids[:, None] == block_ids[None, :])

    def tail_part(inputs):
        key_rows, value_rows, block_ids = inputs
        weight = (block_ids == block_ids[TOK_DEV - 1]).astype(jnp.float32)[:, None, None]
        return jnp.einsum('shd,she->hde', key_rows.astype(jnp.float32) * weight, value_rows.astype(jnp.float32))
    tails = lax.map(tail_part, (key_blocks, value_blocks, id_blocks))
    befores = jnp.einsum('ij,jhde->ihde', upward, tails, precision=lax.Precision.HIGHEST)

    def middle(inputs):
        query_rows, key_rows, value_rows, gate_rows, grad_rows, block_ids, before, before_id = inputs
        scores = masked_scores(query_rows, key_rows, causal_of(block_ids))
        head_hit = (block_ids == before_id).astype(jnp.float32)[:, None, None]
        attended = jnp.einsum('hts,she->the', scores.astype(jnp.float32), value_rows.astype(jnp.float32))
        attended = attended + head_hit * jnp.einsum('thd,hde->the', query_rows.astype(jnp.float32), widen(before))
        gate_open = jax.nn.sigmoid(gate_rows.astype(jnp.float32))
        upstream = grad_rows.astype(jnp.float32) * gate_open
        square_sum = lax.optimization_barrier(jnp.sum(attended * attended, axis=(1, 2)))
        cross_sum = lax.optimization_barrier(jnp.sum(upstream * attended, axis=(1, 2)))
        inverse = lax.rsqrt(square_sum / feature_total + EPSILON)
        normed = attended * inverse[:, None, None]
        gate_grad = (grad_rows.astype(jnp.float32) * normed * gate_open * (1.0 - gate_open)).astype(jnp.bfloat16)
        factor = inverse * inverse * inverse * cross_sum / feature_total
        out_grad = (upstream * inverse[:, None, None] - attended * factor[:, None, None]).astype(jnp.bfloat16)
        lead = (block_ids == block_ids[0]).astype(jnp.float32)[:, None, None]
        lead_state = jnp.einsum('thd,the->hde', query_rows.astype(jnp.float32) * lead, out_grad.astype(jnp.float32))
        return (gate_grad, out_grad, lead_state)
    gate_grads, out_grads, leads = lax.map(middle, (query_blocks, key_blocks, value_blocks, gate_blocks, grad_blocks, id_blocks, befores, previous))
    afters = jnp.einsum('ij,jhde->ihde', downward, leads, precision=lax.Precision.HIGHEST)

    def finish(inputs):
        query_rows, key_rows, value_rows, block_ids, out_grad, before, before_id, after, after_id = inputs
        causal = causal_of(block_ids)
        scores = masked_scores(query_rows, key_rows, causal).astype(jnp.float32)
        back_scores = masked_scores(out_grad, value_rows, causal).astype(jnp.float32)
        head_hit = (block_ids == before_id).astype(jnp.float32)[:, None, None]
        tail_hit = (block_ids == after_id).astype(jnp.float32)[:, None, None]
        grad_f = out_grad.astype(jnp.float32)
        query_f = query_rows.astype(jnp.float32)
        key_f = key_rows.astype(jnp.float32)
        value_f = value_rows.astype(jnp.float32)
        before_w = widen(before)
        after_w = widen(after)
        query_grad = jnp.einsum('hts,shd->thd', back_scores, key_f) + head_hit * jnp.einsum('the,hde->thd', grad_f, before_w)
        key_grad = jnp.einsum('hts,thd->shd', back_scores, query_f) + tail_hit * jnp.einsum('she,hde->shd', value_f, after_w)
        value_grad = jnp.einsum('hts,the->she', scores, grad_f) + tail_hit * jnp.einsum('shd,hde->she', key_f, after_w)
        return (query_grad.astype(jnp.bfloat16), key_grad.astype(jnp.bfloat16), value_grad.astype(jnp.bfloat16))
    query_grads, key_grads, value_grads = lax.map(finish, (query_blocks, key_blocks, value_blocks, id_blocks, out_grads, befores, previous, afters, following))
    flat_shape = (TOKENS, feature_total)
    return (query_grads.reshape(flat_shape), key_grads.reshape(flat_shape), value_grads.reshape(flat_shape), gate_grads.reshape(flat_shape))
```

```python
import functools

import jax
import jax.numpy as jnp
from jax import lax
from jax.experimental import pallas as pl
from jax.experimental.pallas import tpu as pltpu
from jax.sharding import PartitionSpec as P

HEADS = 32
HEAD = 128
EPSILON = 1e-06
FEATURES = HEADS * HEAD
BF = jnp.bfloat16
F32 = jnp.float32
IDS = 16
MIB = 1 << 20


def dot(a, b, dims):
    return lax.dot_general(a, b, (dims, ((), ())), preferred_element_type=F32)


NN = ((1,), (0,))
NT = ((1,), (1,))
TN = ((0,), (0,))


def head(h):
    return slice(h * HEAD, (h + 1) * HEAD)


def column(row, lanes):
    return jnp.broadcast_to(row, (lanes, row.shape[1])).T


def put_ids(ids, out_ref, states):
    last = jnp.broadcast_to(ids[:, -1:], (IDS, HEAD))
    first = jnp.broadcast_to(ids[:, :1], (IDS, HEAD))
    out_ref[states : states + IDS, :] = last.astype(F32).astype(BF)
    out_ref[states + IDS :, :] = first.astype(F32).astype(BF)


def tail_kernel(ids_ref, k_ref, v_ref, out_ref):
    ids = ids_ref[...]
    states = k_ref.shape[1]
    hit = (column(ids, HEAD) == ids[:, -1:]).astype(F32).astype(BF)
    for h in range(states // HEAD):
        state = dot(k_ref[:, head(h)] * hit, v_ref[:, head(h)], TN)
        out_ref[head(h), :] = state.astype(BF)
    put_ids(ids, out_ref, states)


def local_kernel(ids_ref, q_ref, k_ref, v_ref, g_ref, c_ref, scores_ref, local_ref, up_ref):
    ids = ids_ref[...]
    length = ids.shape[1]
    at = lax.broadcasted_iota(jnp.int32, (length, length), 0)
    of = lax.broadcasted_iota(jnp.int32, (length, length), 1)
    causal = (of <= at) & (column(ids, length) == ids)
    for h in range(q_ref.shape[1] // HEAD):
        scores = dot(q_ref[:, head(h)], k_ref[:, head(h)], NT)
        scores = jnp.where(causal, scores, 0.0).astype(BF)
        scores_ref[h] = scores
        local_ref[:, head(h)] = dot(scores, v_ref[:, head(h)], NN)
        gate = jax.nn.sigmoid(g_ref[:, head(h)].astype(F32))
        up_ref[:, head(h)] = c_ref[:, head(h)].astype(F32) * gate


def attend_kernel(ids_ref, q_ref, before_ref, local_ref, up_ref, attended_ref, sums_ref):
    ids = ids_ref[...]
    length = ids.shape[1]
    hit = (column(ids, HEAD) == ids[:, :1]).astype(F32).astype(BF)
    square = jnp.zeros((length, HEAD), F32)
    cross = jnp.zeros((length, HEAD), F32)
    for h in range(q_ref.shape[1] // HEAD):
        attended = local_ref[:, head(h)] + dot(q_ref[:, head(h)] * hit, before_ref[head(h), :], NN)
        attended_ref[:, head(h)] = attended
        square = square + attended * attended
        cross = cross + up_ref[:, head(h)] * attended
    sums_ref[0:1, :] = jnp.sum(square.T, axis=0, keepdims=True)
    sums_ref[1:2, :] = jnp.sum(cross.T, axis=0, keepdims=True)


def scales(parts):
    total = parts[0][...]
    for part in parts[1:]:
        total = total + part[...]
    inverse = lax.rsqrt(total[0:1, :] / FEATURES + EPSILON)
    factor = inverse * inverse * inverse * total[1:2, :] / FEATURES
    return inverse, factor


def lead_kernel(ids_ref, s0, s1, s2, s3, q_ref, attended_ref, up_ref, grad_ref, out_ref):
    ids = ids_ref[...]
    states = q_ref.shape[1]
    inverse, factor = scales((s0, s1, s2, s3))
    inverse, factor = column(inverse, HEAD), column(factor, HEAD)
    hit = (column(ids, HEAD) == ids[:, :1]).astype(F32).astype(BF)
    for h in range(states // HEAD):
        grad = up_ref[:, head(h)] * inverse - attended_ref[:, head(h)] * factor
        grad = grad.astype(BF)
        grad_ref[:, head(h)] = grad
        out_ref[head(h), :] = dot(q_ref[:, head(h)] * hit, grad, TN).astype(BF)
    put_ids(ids, out_ref, states)


def back_kernel(
    ids_ref, s0, s1, s2, s3, q_ref, k_ref, v_ref, g_ref, scores_ref, attended_ref, up_ref, grad_ref, before_ref,
    query_grad_ref, gate_grad_ref, key_part_ref, value_part_ref,
):
    ids = ids_ref[...]
    length = ids.shape[1]
    inverse, _ = scales((s0, s1, s2, s3))
    inverse = column(inverse, HEAD)
    hit = (column(ids, HEAD) == ids[:, :1]).astype(F32).astype(BF)
    at = lax.broadcasted_iota(jnp.int32, (length, length), 0)
    of = lax.broadcasted_iota(jnp.int32, (length, length), 1)
    causal = (of <= at) & (column(ids, length) == ids)
    for h in range(q_ref.shape[1] // HEAD):
        grad = grad_ref[:, head(h)]
        back = jnp.where(causal, dot(grad, v_ref[:, head(h)], NT), 0.0).astype(BF)
        query_grad = dot(back, k_ref[:, head(h)], NN) + dot(grad * hit, before_ref[head(h), :], NT)
        query_grad_ref[:, head(h)] = query_grad.astype(BF)
        key_part_ref[:, head(h)] = dot(back, q_ref[:, head(h)], TN)
        value_part_ref[:, head(h)] = dot(scores_ref[h], grad, TN)
        gate = jax.nn.sigmoid(g_ref[:, head(h)].astype(F32))
        gate_grad = up_ref[:, head(h)] * attended_ref[:, head(h)] * inverse * (1.0 - gate)
        gate_grad_ref[:, head(h)] = gate_grad.astype(BF)


def finish_kernel(ids_ref, k_ref, v_ref, after_ref, key_part_ref, value_part_ref, key_grad_ref, value_grad_ref):
    ids = ids_ref[...]
    hit = (column(ids, HEAD) == ids[:, -1:]).astype(F32).astype(BF)
    for h in range(k_ref.shape[1] // HEAD):
        after = after_ref[head(h), :]
        key_grad = key_part_ref[:, head(h)] + dot(v_ref[:, head(h)] * hit, after, NT)
        key_grad_ref[:, head(h)] = key_grad.astype(BF)
        value_grad = value_part_ref[:, head(h)] + dot(k_ref[:, head(h)] * hit, after, NN)
        value_grad_ref[:, head(h)] = value_grad.astype(BF)


def call(kernel, outs, flops, *args):
    whole = pl.BlockSpec(memory_space=pltpu.VMEM)
    size = sum(a.size * a.dtype.itemsize for a in (*args, *outs))
    return pl.pallas_call(
        kernel,
        out_shape=outs,
        in_specs=[whole] * len(args),
        out_specs=[whole] * len(outs),
        compiler_params=pltpu.CompilerParams(vmem_limit_bytes=24 * MIB),
        cost_estimate=pl.CostEstimate(flops=flops, bytes_accessed=size, transcendentals=0),
        name=kernel.__name__,
    )(*args)


def body(queries, keys, values, gates, cotangent, doc_ids):
    length, states = queries.shape
    count = lax.axis_size("ctx")
    heads = states // HEAD
    shape = jax.ShapeDtypeStruct
    ids = doc_ids.reshape(1, length)
    odd = lax.rem(lax.axis_index("ctx"), 2) == 1
    message = shape((states + 2 * IDS, HEAD), BF)
    wide = shape((length, states), F32)
    narrow = shape((length, states), BF)
    unit = 2 * length * length * states

    def swap(x):
        return lax.ppermute(x, "ctx", [(i, i ^ 1) for i in range(count)])

    def spread(x, way):
        pairs = [(i, (i + way * (2 if i % 2 == 0 else 4)) % count) for i in range(count)]
        return lax.ppermute(x, "ctx", pairs)

    def add(a, b):
        return (a.astype(F32) + b.astype(F32)).astype(BF)

    is_state = lax.broadcasted_iota(jnp.int32, message.shape, 0) < states

    def last_of(m):
        return m[states, 0]

    def first_of(m):
        return m[states + IDS, 0]

    (mine,) = call(tail_kernel, [message], unit // 2, ids, keys, values)
    theirs = swap(mine)
    even_part, odd_part = jnp.where(odd, theirs, mine), jnp.where(odd, mine, theirs)
    first_even, last_even = first_of(even_part), last_of(even_part)
    first_odd, last_odd = first_of(odd_part), last_of(odd_part)
    chip = jnp.where(is_state & (last_even == last_odd), add(mine, theirs), odd_part)
    came = spread(chip, 1)
    scores, local, up = call(
        local_kernel, [shape((heads, length, length), BF), wide, wide], 2 * unit, ids, queries, keys, values, gates, cotangent
    )
    came = jnp.where(last_of(came) == first_even, came[:states], 0)
    entering = add(came, swap(came))
    before = jnp.where(
        odd,
        jnp.where(
            first_odd == last_even,
            jnp.where(first_even == last_even, add(even_part[:states], entering), even_part[:states]),
            0,
        ),
        entering,
    )
    attended, sums = call(attend_kernel, [wide, shape((2, length), F32)], unit // 2, ids, queries, before, local, up)
    ranks = lax.axis_size("tp")
    parts = [sums] + [
        lax.ppermute(sums, "tp", [(i, (i + step) % ranks) for i in range(ranks)]) for step in (2, 1, 3)
    ]
    grad, lead = call(lead_kernel, [narrow, message], unit // 2, ids, *parts, queries, attended, up)

    other = swap(lead)
    lead_even, lead_odd = jnp.where(odd, other, lead), jnp.where(odd, lead, other)
    chip = jnp.where(is_state & (first_even == first_odd), add(lead, other), lead_even)
    came = spread(chip, -1)
    query_grad, gate_grad, key_part, value_part = call(
        back_kernel, [narrow, narrow, wide, wide], 5 * unit, ids, *parts, queries, keys, values, gates, scores, attended,
        up, grad, before,
    )
    came = jnp.where(first_of(came) == last_odd, came[:states], 0)
    leaving = add(came, swap(came))
    after = jnp.where(
        odd,
        leaving,
        jnp.where(
            first_odd == last_even,
            jnp.where(first_odd == last_odd, add(lead_odd[:states], leaving), lead_odd[:states]),
            0,
        ),
    )
    key_grad, value_grad = call(finish_kernel, [narrow, narrow], unit, ids, keys, values, after, key_part, value_part)
    return query_grad, key_grad, value_grad, gate_grad


def solution(mesh):
    return jax.shard_map(
        body,
        mesh=mesh,
        in_specs=(P("ctx", "tp"),) * 5 + (P("ctx"),),
        out_specs=(P("ctx", "tp"),) * 4,
        check_vma=False,
    )
```

```python
import functools

import jax
import jax.numpy as jnp
from jax import lax
from jax.experimental import pallas as pl
from jax.experimental.pallas import tpu as pltpu
from jax.sharding import PartitionSpec as P

HEADS = 32
HEAD = 128
EPSILON = 1e-06
FEATURES = HEADS * HEAD
BF = jnp.bfloat16
F32 = jnp.float32
IDS = 16
MIB = 1 << 20


def dot(a, b, dims):
    return lax.dot_general(a, b, (dims, ((), ())), preferred_element_type=F32)


NN = ((1,), (0,))
NT = ((1,), (1,))
TN = ((0,), (0,))


def head(h):
    return slice(h * HEAD, (h + 1) * HEAD)


def column(row, lanes):
    return jnp.broadcast_to(row, (lanes, row.shape[1])).T


def put_ids(ids, out_ref, states):
    last = jnp.broadcast_to(ids[:, -1:], (IDS, HEAD))
    first = jnp.broadcast_to(ids[:, :1], (IDS, HEAD))
    out_ref[states : states + IDS, :] = last.astype(F32).astype(BF)
    out_ref[states + IDS :, :] = first.astype(F32).astype(BF)


def last_of(message_ref):
    states = message_ref.shape[0] - 2 * IDS
    return message_ref[states : states + IDS, :].astype(F32)[:1]


def first_of(message_ref):
    states = message_ref.shape[0] - 2 * IDS
    return message_ref[states + IDS :, :].astype(F32)[:1]


def tail_kernel(ids_hbm, k_hbm, v_hbm, out_ref, ids_ref, k_ref, v_ref, ids_sem, k_sem, v_sem):
    states = k_ref.shape[1]
    heads = range(states // HEAD)
    ids_copy = pltpu.make_async_copy(ids_hbm, ids_ref, ids_sem)
    k_copies = [pltpu.make_async_copy(k_hbm.at[:, head(h)], k_ref.at[:, head(h)], k_sem.at[h]) for h in heads]
    v_copies = [pltpu.make_async_copy(v_hbm.at[:, head(h)], v_ref.at[:, head(h)], v_sem.at[h]) for h in heads]
    ids_copy.start()
    for h in heads:
        k_copies[h].start()
        v_copies[h].start()
    ids_copy.wait()
    ids = ids_ref[...]
    hit = (column(ids, HEAD) == ids[:, -1:]).astype(F32).astype(BF)
    put_ids(ids, out_ref, states)
    for h in heads:
        k_copies[h].wait()
        v_copies[h].wait()
        state = dot(k_ref[:, head(h)] * hit, v_ref[:, head(h)], TN)
        out_ref[head(h), :] = state.astype(BF)


def chip_kernel(backward, odd_ref, mine_ref, theirs_ref, out_ref):
    states = out_ref.shape[0] - 2 * IDS
    odd = odd_ref[...] > 0
    kept = ~odd if backward else odd
    part = first_of if backward else last_of
    both = part(mine_ref) == part(theirs_ref)
    for rows in (*(head(h) for h in range(states // HEAD)), slice(states, states + 2 * IDS)):
        mine, theirs = mine_ref[rows, :].astype(F32), theirs_ref[rows, :].astype(F32)
        chosen = jnp.where(kept, mine, theirs)
        if rows.start < states:
            chosen = jnp.where(both, mine + theirs, chosen)
        out_ref[rows, :] = chosen.astype(BF)


def joined(backward, odd_ref, mine_ref, theirs_ref, came_ref, other_ref):
    odd = odd_ref[...] > 0
    part = first_of if backward else last_of
    far = last_of if backward else first_of
    inner = ~odd if backward else odd
    mine_near, mine_far = part(mine_ref), far(mine_ref)
    theirs_near, theirs_far = part(theirs_ref), far(theirs_ref)
    edge = jnp.where(inner, theirs_far, mine_far)
    take_came, take_other = part(came_ref) == edge, part(other_ref) == edge
    take_theirs = inner & (theirs_near == mine_far)
    take_outer = ~inner | (take_theirs & (theirs_near == theirs_far))

    def rows_of(rows):
        outer = jnp.where(take_came, came_ref[rows, :].astype(F32), 0.0)
        outer = outer + jnp.where(take_other, other_ref[rows, :].astype(F32), 0.0)
        own = jnp.where(take_theirs, theirs_ref[rows, :].astype(F32), 0.0)
        return (own + jnp.where(take_outer, outer, 0.0)).astype(BF)

    return rows_of


def local_kernel(ids_ref, q_ref, k_ref, v_ref, g_ref, c_ref, scores_ref, local_ref, up_ref):
    ids = ids_ref[...]
    length = ids.shape[1]
    at = lax.broadcasted_iota(jnp.int32, (length, length), 0)
    of = lax.broadcasted_iota(jnp.int32, (length, length), 1)
    causal = (of <= at) & (column(ids, length) == ids)
    for h in range(q_ref.shape[1] // HEAD):
        scores = dot(q_ref[:, head(h)], k_ref[:, head(h)], NT)
        scores = jnp.where(causal, scores, 0.0).astype(BF)
        scores_ref[h] = scores
        local_ref[:, head(h)] = dot(scores, v_ref[:, head(h)], NN)
        gate = jax.nn.sigmoid(g_ref[:, head(h)].astype(F32))
        up_ref[:, head(h)] = c_ref[:, head(h)].astype(F32) * gate


def attend_kernel(
    ids_ref, odd_ref, mine_ref, theirs_ref, came_ref, other_ref, q_ref, local_ref, up_ref,
    before_ref, attended_ref, sums_ref,
):
    ids = ids_ref[...]
    length = ids.shape[1]
    entering = joined(False, odd_ref, mine_ref, theirs_ref, came_ref, other_ref)
    hit = (column(ids, HEAD) == ids[:, :1]).astype(F32).astype(BF)
    square = jnp.zeros((length, HEAD), F32)
    cross = jnp.zeros((length, HEAD), F32)
    for h in range(q_ref.shape[1] // HEAD):
        before = entering(head(h))
        before_ref[head(h), :] = before
        attended = local_ref[:, head(h)] + dot(q_ref[:, head(h)] * hit, before, NN)
        attended_ref[:, head(h)] = attended
        square = square + attended * attended
        cross = cross + up_ref[:, head(h)] * attended
    sums_ref[0:1, :] = jnp.sum(square.T, axis=0, keepdims=True)
    sums_ref[1:2, :] = jnp.sum(cross.T, axis=0, keepdims=True)


def scales(parts):
    total = parts[0][...]
    for part in parts[1:]:
        total = total + part[...]
    inverse = lax.rsqrt(total[0:1, :] / FEATURES + EPSILON)
    factor = inverse * inverse * inverse * total[1:2, :] / FEATURES
    return inverse, factor


def lead_kernel(ids_ref, s0, s1, s2, s3, q_ref, attended_ref, up_ref, grad_ref, out_ref):
    ids = ids_ref[...]
    states = q_ref.shape[1]
    inverse, factor = scales((s0, s1, s2, s3))
    inverse, factor = column(inverse, HEAD), column(factor, HEAD)
    hit = (column(ids, HEAD) == ids[:, :1]).astype(F32).astype(BF)
    for h in range(states // HEAD):
        grad = up_ref[:, head(h)] * inverse - attended_ref[:, head(h)] * factor
        grad = grad.astype(BF)
        grad_ref[:, head(h)] = grad
        out_ref[head(h), :] = dot(q_ref[:, head(h)] * hit, grad, TN).astype(BF)
    put_ids(ids, out_ref, states)


def back_kernel(
    ids_ref, s0, s1, s2, s3, q_ref, k_ref, v_ref, g_ref, scores_ref, attended_ref, up_ref, grad_ref, before_ref,
    query_grad_ref, gate_grad_ref, key_part_ref, value_part_ref,
):
    ids = ids_ref[...]
    length = ids.shape[1]
    inverse, _ = scales((s0, s1, s2, s3))
    inverse = column(inverse, HEAD)
    hit = (column(ids, HEAD) == ids[:, :1]).astype(F32).astype(BF)
    at = lax.broadcasted_iota(jnp.int32, (length, length), 0)
    of = lax.broadcasted_iota(jnp.int32, (length, length), 1)
    causal = (of <= at) & (column(ids, length) == ids)
    for h in range(q_ref.shape[1] // HEAD):
        grad = grad_ref[:, head(h)]
        back = jnp.where(causal, dot(grad, v_ref[:, head(h)], NT), 0.0).astype(BF)
        query_grad = dot(back, k_ref[:, head(h)], NN) + dot(grad * hit, before_ref[head(h), :], NT)
        query_grad_ref[:, head(h)] = query_grad.astype(BF)
        key_part_ref[:, head(h)] = dot(back, q_ref[:, head(h)], TN)
        value_part_ref[:, head(h)] = dot(scores_ref[h], grad, TN)
        gate = jax.nn.sigmoid(g_ref[:, head(h)].astype(F32))
        gate_grad = up_ref[:, head(h)] * attended_ref[:, head(h)] * inverse * (1.0 - gate)
        gate_grad_ref[:, head(h)] = gate_grad.astype(BF)


def finish_kernel(
    ids_ref, odd_ref, mine_ref, theirs_ref, came_ref, other_ref, k_ref, v_ref, key_part_ref, value_part_ref,
    key_grad_hbm, value_grad_hbm, key_grad_ref, value_grad_ref, key_sem, value_sem,
):
    ids = ids_ref[...]
    leaving = joined(True, odd_ref, mine_ref, theirs_ref, came_ref, other_ref)
    hit = (column(ids, HEAD) == ids[:, -1:]).astype(F32).astype(BF)
    copies = []
    for h in range(k_ref.shape[1] // HEAD):
        after = leaving(head(h))
        key_grad = key_part_ref[:, head(h)] + dot(v_ref[:, head(h)] * hit, after, NT)
        key_grad_ref[:, head(h)] = key_grad.astype(BF)
        copies.append(pltpu.make_async_copy(key_grad_ref.at[:, head(h)], key_grad_hbm.at[:, head(h)], key_sem.at[h]))
        copies[-1].start()
        value_grad = value_part_ref[:, head(h)] + dot(k_ref[:, head(h)] * hit, after, NN)
        value_grad_ref[:, head(h)] = value_grad.astype(BF)
        copies.append(
            pltpu.make_async_copy(value_grad_ref.at[:, head(h)], value_grad_hbm.at[:, head(h)], value_sem.at[h])
        )
        copies[-1].start()
    for copy in copies:
        copy.wait()


VMEM = pl.BlockSpec(memory_space=pltpu.VMEM)
HBM = pl.BlockSpec(memory_space=pltpu.HBM)


def call(kernel, outs, flops, *args, name=None, in_specs=None, out_specs=None, scratch=(), vmem=24 * MIB):
    size = sum(a.size * a.dtype.itemsize for a in (*args, *outs))
    return pl.pallas_call(
        kernel,
        out_shape=outs,
        in_specs=in_specs or [VMEM] * len(args),
        out_specs=out_specs or [VMEM] * len(outs),
        scratch_shapes=scratch,
        compiler_params=pltpu.CompilerParams(vmem_limit_bytes=vmem),
        cost_estimate=pl.CostEstimate(flops=flops, bytes_accessed=size, transcendentals=0),
        name=name or kernel.__name__,
    )(*args)


def body(queries, keys, values, gates, cotangent, doc_ids):
    length, states = queries.shape
    count, ranks = lax.axis_size("ctx"), lax.axis_size("tp")
    heads = states // HEAD
    shape = jax.ShapeDtypeStruct
    ids = doc_ids.reshape(1, length)
    odd = jnp.broadcast_to(lax.rem(lax.axis_index("ctx"), 2), (1, HEAD))
    message = shape((states + 2 * IDS, HEAD), BF)
    wide = shape((length, states), F32)
    narrow = shape((length, states), BF)
    unit = 2 * length * length * states
    buffer, sems = pltpu.VMEM((length, states), BF), pltpu.SemaphoreType.DMA((heads,))

    def swap(x):
        return lax.ppermute(x, "ctx", [(i, i ^ 1) for i in range(count)])

    def spread(x, way):
        pairs = [(i, (i + way * (2 if i % 2 == 0 else 4)) % count) for i in range(count)]
        return lax.ppermute(x, "ctx", pairs)

    (tail,) = call(
        tail_kernel, [message], unit // 2, ids, keys, values, in_specs=[HBM] * 3,
        scratch=[pltpu.VMEM((1, length), jnp.int32), buffer, buffer, pltpu.SemaphoreType.DMA, sems, sems], vmem=int(53.5 * MIB),
    )
    tail_other = swap(tail)
    (chip,) = call(functools.partial(chip_kernel, False), [message], 0, odd, tail, tail_other, name="chip_tail")
    came = spread(chip, 1)
    ids, _ = lax.optimization_barrier((ids, chip))
    scores, local, up = call(
        local_kernel, [shape((heads, length, length), BF), wide, wide], 2 * unit, ids, queries, keys, values, gates, cotangent
    )
    came, local = lax.optimization_barrier((came, local))
    other = swap(came)
    before, attended, sums = call(
        attend_kernel, [shape((states, HEAD), BF), wide, shape((2, length), F32)], unit // 2,
        ids, odd, tail, tail_other, came, other, queries, local, up,
    )
    parts = [sums] + [
        lax.ppermute(sums, "tp", [(i, (i + step) % ranks) for i in range(ranks)]) for step in (2, 1, 3)
    ]
    grad, lead = call(lead_kernel, [narrow, message], unit // 2, ids, *parts, queries, attended, up)

    lead_other = swap(lead)
    (chip,) = call(functools.partial(chip_kernel, True), [message], 0, odd, lead, lead_other, name="chip_lead")
    came = spread(chip, -1)
    ids, _ = lax.optimization_barrier((ids, chip))
    query_grad, gate_grad, key_part, value_part = call(
        back_kernel, [narrow, narrow, wide, wide], 5 * unit, ids, *parts, queries, keys, values, gates, scores, attended,
        up, grad, before,
    )
    came, key_part = lax.optimization_barrier((came, key_part))
    other = swap(came)
    key_grad, value_grad = call(
        finish_kernel, [narrow, narrow], unit, ids, odd, lead, lead_other, came, other, keys, values, key_part, value_part,
        out_specs=[HBM] * 2, scratch=[buffer, buffer, sems, sems],
    )
    return query_grad, key_grad, value_grad, gate_grad


def solution(mesh):
    return jax.shard_map(
        body,
        mesh=mesh,
        in_specs=(P("ctx", "tp"),) * 5 + (P("ctx"),),
        out_specs=(P("ctx", "tp"),) * 4,
        check_vma=False,
    )
```

```python
import functools

import jax
import jax.numpy as jnp
from jax import lax
from jax.experimental import pallas as pl
from jax.experimental.pallas import tpu as pltpu
from jax.sharding import PartitionSpec as P

HEADS = 32
HEAD = 128
EPSILON = 1e-06
FEATURES = HEADS * HEAD
BF = jnp.bfloat16
F32 = jnp.float32
IDS = 8
MIB = 1 << 20


def dot(a, b, dims):
    return lax.dot_general(a, b, (dims, ((), ())), preferred_element_type=F32)


NN = ((1,), (0,))
NT = ((1,), (1,))
TN = ((0,), (0,))


def head(h):
    return slice(h * HEAD, (h + 1) * HEAD)


def column(row, lanes):
    return jnp.broadcast_to(row, (lanes, row.shape[1])).T


def put_ids(ids, out_ref):
    last = jnp.broadcast_to(ids[:, -1:], (IDS, HEAD))
    first = jnp.broadcast_to(ids[:, :1], (IDS, HEAD))
    out_ref[-2 * IDS :, :] = jnp.concatenate([last, first]).astype(F32).astype(BF)


def get_ids(message_ref):
    ids = message_ref[-2 * IDS :, :].astype(F32)
    return ids[:1], ids[IDS : IDS + 1]


def load_kernel(k_hbm, v_hbm, k_ref, v_ref, sems):
    k_copy = pltpu.make_async_copy(k_hbm, k_ref, sems.at[0])
    v_copy = pltpu.make_async_copy(v_hbm, v_ref, sems.at[1])
    k_copy.start()
    v_copy.start()
    k_copy.wait()
    v_copy.wait()


def split(states, odd, keep_ref, send_ref):
    half = len(states) // 2
    for h in range(half):
        keep_ref[head(h), :] = jnp.where(odd, states[half + h], states[h]).astype(BF)
        send_ref[head(h), :] = jnp.where(odd, states[h], states[half + h]).astype(BF)


def tail_kernel(ids_ref, odd_ref, k_ref, v_ref, keep_ref, send_ref):
    ids = ids_ref[...]
    hit = (column(ids, HEAD) == ids[:, -1:]).astype(F32).astype(BF)
    put_ids(ids, send_ref)
    heads = range(k_ref.shape[1] // HEAD)
    states = [dot(k_ref[:, head(h)] * hit, v_ref[:, head(h)], TN) for h in heads]
    split(states, odd_ref[...] > 0, keep_ref, send_ref)


def chip_kernel(backward, odd_ref, keep_ref, send_ref, theirs_ref, out_ref):
    odd = odd_ref[...] > 0
    mine_kept = ~odd if backward else odd
    which = 1 if backward else 0
    both = get_ids(send_ref)[which] == get_ids(theirs_ref)[which]
    for h in range(keep_ref.shape[0] // HEAD):
        mine, theirs = keep_ref[head(h), :].astype(F32), theirs_ref[head(h), :].astype(F32)
        state = jnp.where(both, mine + theirs, jnp.where(mine_kept, mine, theirs))
        out_ref[head(h), :] = state.astype(BF)
    mine, theirs = send_ref[-2 * IDS :, :].astype(F32), theirs_ref[-2 * IDS :, :].astype(F32)
    out_ref[-2 * IDS :, :] = jnp.where(mine_kept, mine, theirs).astype(BF)


def edge_kernel(backward, odd_ref, keep_ref, send_ref, theirs_ref, near_ref, far_ref, mine_ref, other_ref):
    odd = odd_ref[...] > 0
    inner = ~odd if backward else odd
    which, opposite = (1, 0) if backward else (0, 1)
    ours, others = get_ids(send_ref), get_ids(theirs_ref)
    outer_part = jnp.where(inner, others[which], ours[which])
    outer_edge = jnp.where(inner, others[opposite], ours[opposite])
    inner_edge = jnp.where(inner, ours[opposite], others[opposite])
    take_near = get_ids(near_ref)[which] == outer_edge
    take_far = get_ids(far_ref)[which] == outer_edge
    take_part = inner_edge == outer_part
    take_outer = take_part & (outer_part == outer_edge)
    for h in range(keep_ref.shape[0] // HEAD):
        outer = jnp.where(take_near, near_ref[head(h), :].astype(F32), 0.0)
        outer = outer + jnp.where(take_far, far_ref[head(h), :].astype(F32), 0.0)
        part = jnp.where(inner, theirs_ref[head(h), :].astype(F32), keep_ref[head(h), :].astype(F32))
        joined = jnp.where(take_part, part, 0.0) + jnp.where(take_outer, outer, 0.0)
        mine_ref[head(h), :] = jnp.where(inner, joined, outer).astype(BF)
        other_ref[head(h), :] = jnp.where(inner, outer, joined).astype(BF)


def merged(odd_ref, mine_ref, other_ref):
    odd = odd_ref[...] > 0
    half = mine_ref.shape[0] // HEAD

    def state(h):
        mine, other = mine_ref[head(h % half), :].astype(F32), other_ref[head(h % half), :].astype(F32)
        return (jnp.where(odd, other, mine) if h < half else jnp.where(odd, mine, other)).astype(BF)

    return state


def local_kernel(
    ids_ref, q_ref, k_ref, v_ref, g_ref, c_ref, scores_ref, local_ref, up_ref, lead_q_ref, lead_qt_ref
):
    ids = ids_ref[...]
    length = ids.shape[1]
    at = lax.broadcasted_iota(jnp.int32, (length, length), 0)
    of = lax.broadcasted_iota(jnp.int32, (length, length), 1)
    causal = (of <= at) & (column(ids, length) == ids)
    hit = (column(ids, HEAD) == ids[:, :1]).astype(F32)
    for h in range(q_ref.shape[1] // HEAD):
        scores = dot(q_ref[:, head(h)], k_ref[:, head(h)], NT)
        scores = jnp.where(causal, scores, 0.0).astype(BF)
        scores_ref[h] = scores
        local_ref[:, head(h)] = dot(scores, v_ref[:, head(h)], NN)
        gate = jax.nn.sigmoid(g_ref[:, head(h)].astype(F32))
        up_ref[:, head(h)] = c_ref[:, head(h)].astype(F32) * gate
        lead_q = q_ref[:, head(h)].astype(F32) * hit
        lead_q_ref[:, head(h)] = lead_q.astype(BF)
        lead_qt_ref[head(h), :] = lead_q.T.astype(BF)


def attend_kernel(odd_ref, mine_ref, other_ref, lead_q_ref, local_ref, up_ref, before_ref, attended_ref, sums_ref):
    length, states = lead_q_ref.shape
    entering = merged(odd_ref, mine_ref, other_ref)
    square = jnp.zeros((length, HEAD), F32)
    cross = jnp.zeros((length, HEAD), F32)
    for h in range(states // HEAD):
        before = entering(h)
        before_ref[head(h), :] = before
        attended = local_ref[:, head(h)] + dot(lead_q_ref[:, head(h)], before, NN)
        attended_ref[:, head(h)] = attended
        square = square + attended * attended
        cross = cross + up_ref[:, head(h)] * attended
    sums_ref[0:1, :] = jnp.sum(square.T, axis=0, keepdims=True)
    sums_ref[1:2, :] = jnp.sum(cross.T, axis=0, keepdims=True)


def scales(parts):
    total = parts[0][...]
    for part in parts[1:]:
        total = total + part[...]
    inverse = lax.rsqrt(total[0:1, :] / FEATURES + EPSILON)
    factor = inverse * inverse * inverse * total[1:2, :] / FEATURES
    return inverse, factor


def lead_kernel(ids_ref, odd_ref, s0, s1, s2, s3, lead_qt_ref, attended_ref, up_ref, grad_ref, keep_ref, send_ref):
    inverse, factor = scales((s0, s1, s2, s3))
    inverse, factor = column(inverse, HEAD), column(factor, HEAD)
    put_ids(ids_ref[...], send_ref)
    states = []
    for h in range(up_ref.shape[1] // HEAD):
        grad = up_ref[:, head(h)] * inverse - attended_ref[:, head(h)] * factor
        grad = grad.astype(BF)
        grad_ref[:, head(h)] = grad
        states.append(dot(lead_qt_ref[head(h), :], grad, NN))
    split(states, odd_ref[...] > 0, keep_ref, send_ref)


def back_kernel(
    ids_ref, s0, s1, s2, s3, q_ref, k_ref, v_ref, g_ref, scores_ref, attended_ref, up_ref, grad_ref, before_ref,
    query_grad_ref, gate_grad_ref, key_part_ref, value_part_ref, tail_k_ref, tail_v_ref,
):
    ids = ids_ref[...]
    length = ids.shape[1]
    inverse, _ = scales((s0, s1, s2, s3))
    inverse = column(inverse, HEAD)
    hit = (column(ids, HEAD) == ids[:, :1]).astype(F32).astype(BF)
    tail_hit = (column(ids, HEAD) == ids[:, -1:]).astype(F32).astype(BF)
    at = lax.broadcasted_iota(jnp.int32, (length, length), 0)
    of = lax.broadcasted_iota(jnp.int32, (length, length), 1)
    causal = (of <= at) & (column(ids, length) == ids)
    for h in range(q_ref.shape[1] // HEAD):
        grad = grad_ref[:, head(h)]
        back = jnp.where(causal, dot(grad, v_ref[:, head(h)], NT), 0.0).astype(BF)
        query_grad = dot(back, k_ref[:, head(h)], NN) + dot(grad * hit, before_ref[head(h), :], NT)
        query_grad_ref[:, head(h)] = query_grad.astype(BF)
        key_part_ref[:, head(h)] = dot(back, q_ref[:, head(h)], TN)
        value_part_ref[:, head(h)] = dot(scores_ref[h], grad, TN)
        gate = jax.nn.sigmoid(g_ref[:, head(h)].astype(F32))
        gate_grad = up_ref[:, head(h)] * attended_ref[:, head(h)] * inverse * (1.0 - gate)
        gate_grad_ref[:, head(h)] = gate_grad.astype(BF)
        tail_k_ref[:, head(h)] = k_ref[:, head(h)] * tail_hit
        tail_v_ref[:, head(h)] = v_ref[:, head(h)] * tail_hit


def finish_kernel(
    odd_ref, mine_ref, other_ref, tail_k_ref, tail_v_ref, key_part_ref, value_part_ref,
    key_grad_hbm, value_grad_hbm, key_grad_ref, value_grad_ref, key_sem, value_sem,
):
    leaving = merged(odd_ref, mine_ref, other_ref)
    copies = []

    def send(ref, hbm, sem, h):
        copies.append(pltpu.make_async_copy(ref.at[:, head(h)], hbm.at[:, head(h)], sem.at[h]))
        copies[-1].start()

    for h in range(tail_k_ref.shape[1] // HEAD):
        after = leaving(h)
        key_grad = key_part_ref[:, head(h)] + dot(tail_v_ref[:, head(h)], after, NT)
        key_grad_ref[:, head(h)] = key_grad.astype(BF)
        send(key_grad_ref, key_grad_hbm, key_sem, h)
        value_grad = value_part_ref[:, head(h)] + dot(tail_k_ref[:, head(h)], after, NN)
        value_grad_ref[:, head(h)] = value_grad.astype(BF)
        send(value_grad_ref, value_grad_hbm, value_sem, h)
    for copy in copies:
        copy.wait()


VMEM = pl.BlockSpec(memory_space=pltpu.VMEM)
HBM = pl.BlockSpec(memory_space=pltpu.HBM)


def call(kernel, outs, flops, *args, name=None, in_specs=None, out_specs=None, scratch=(), vmem=24 * MIB):
    size = sum(a.size * a.dtype.itemsize for a in (*args, *outs))
    return pl.pallas_call(
        kernel,
        out_shape=outs,
        in_specs=in_specs or [VMEM] * len(args),
        out_specs=out_specs or [VMEM] * len(outs),
        scratch_shapes=scratch,
        compiler_params=pltpu.CompilerParams(vmem_limit_bytes=vmem),
        cost_estimate=pl.CostEstimate(flops=flops, bytes_accessed=size, transcendentals=0),
        name=name or kernel.__name__,
    )(*args)


def body(queries, keys, values, gates, cotangent, doc_ids):
    length, states = queries.shape
    count, ranks = lax.axis_size("ctx"), lax.axis_size("tp")
    heads = states // HEAD
    shape = jax.ShapeDtypeStruct
    ids = doc_ids.reshape(1, length)
    odd = jnp.broadcast_to(lax.rem(lax.axis_index("ctx"), 2), (1, HEAD))
    half = shape((states // 2, HEAD), BF)
    message = shape((states // 2 + 2 * IDS, HEAD), BF)
    wide = shape((length, states), F32)
    narrow = shape((length, states), BF)
    unit = 2 * length * length * states
    buffer, sems = pltpu.VMEM((length, states), BF), pltpu.SemaphoreType.DMA((heads,))

    def swap(x):
        return lax.ppermute(x, "ctx", [(i, i ^ 1) for i in range(count)])

    def shift(x, blocks, wrap=True):
        pairs = [(i, (i + blocks) % count) for i in range(count) if wrap or 0 <= i + blocks < count]
        return lax.ppermute(x, "ctx", pairs)

    def chip(backward, *parts):
        name = "chip_lead" if backward else "chip_tail"
        return call(functools.partial(chip_kernel, backward), [message], 0, odd, *parts, name=name)[0]

    def edge(backward, *parts):
        name = "edge_lead" if backward else "edge_tail"
        return call(functools.partial(edge_kernel, backward), [half, half], 0, odd, *parts, name=name)

    keys, values = call(
        load_kernel, [narrow, narrow], 1, keys, values, in_specs=[HBM] * 2, scratch=[pltpu.SemaphoreType.DMA((2,))],
        vmem=52 * MIB + 768 * 1024,
    )
    tail, tail_sent = call(tail_kernel, [half, message], unit // 2, ids, odd, keys, values)
    tail_theirs = swap(tail_sent)
    state = chip(False, tail, tail_sent, tail_theirs)
    near, far = shift(state, 2, False), shift(state, 4)
    ids, _ = lax.optimization_barrier((ids, state))
    scores, local, up, lead_q, lead_qt = call(
        local_kernel, [shape((heads, length, length), BF), wide, wide, narrow, shape((states, length), BF)], 2 * unit,
        ids, queries, keys, values, gates, cotangent,
    )
    near, far, local = lax.optimization_barrier((near, far, local))
    mine, given = edge(False, tail, tail_sent, tail_theirs, near, far)
    before, attended, sums = call(
        attend_kernel, [shape((states, HEAD), BF), wide, shape((2, length), F32)], unit // 2,
        odd, mine, swap(given), lead_q, local, up,
    )
    parts = [sums] + [lax.ppermute(sums, "tp", [(i, i ^ step) for i in range(ranks)]) for step in (1, 3, 2)]
    grad, lead, lead_sent = call(
        lead_kernel, [narrow, half, message], unit // 2, ids, odd, *parts, lead_qt, attended, up
    )

    lead_theirs = swap(lead_sent)
    state = chip(True, lead, lead_sent, lead_theirs)
    near, far = shift(state, -2), shift(state, -4)
    ids, _ = lax.optimization_barrier((ids, state))
    query_grad, gate_grad, key_part, value_part, tail_k, tail_v = call(
        back_kernel, [narrow, narrow, wide, wide, narrow, narrow], 5 * unit,
        ids, *parts, queries, keys, values, gates, scores, attended, up, grad, before,
    )
    near, far, key_part = lax.optimization_barrier((near, far, key_part))
    mine, given = edge(True, lead, lead_sent, lead_theirs, near, far)
    key_grad, value_grad = call(
        finish_kernel, [narrow, narrow], unit, odd, mine, swap(given), tail_k, tail_v, key_part, value_part,
        out_specs=[HBM] * 2, scratch=[buffer, buffer, sems, sems],
    )
    return query_grad, key_grad, value_grad, gate_grad


def solution(mesh):
    return jax.shard_map(
        body,
        mesh=mesh,
        in_specs=(P("ctx", "tp"),) * 5 + (P("ctx"),),
        out_specs=(P("ctx", "tp"),) * 4,
        check_vma=False,
    )
```

```python
import functools

import jax
import jax.numpy as jnp
from jax import lax
from jax.experimental import pallas as pl
from jax.experimental.pallas import tpu as pltpu
from jax.sharding import PartitionSpec as P

HEADS = 32
HEAD = 128
EPSILON = 1e-06
FEATURES = HEADS * HEAD
BF = jnp.bfloat16
F32 = jnp.float32
IDS = 8
MIB = 1 << 20


def dot(a, b, dims):
    return lax.dot_general(a, b, (dims, ((), ())), preferred_element_type=F32)


NN = ((1,), (0,))
NT = ((1,), (1,))
TN = ((0,), (0,))


def head(h):
    return slice(h * HEAD, (h + 1) * HEAD)


def column(row, lanes):
    return jnp.broadcast_to(row, (lanes, row.shape[1])).T


def put_ids(ids, out_ref):
    last = jnp.broadcast_to(ids[:, -1:], (IDS, HEAD))
    first = jnp.broadcast_to(ids[:, :1], (IDS, HEAD))
    out_ref[-2 * IDS :, :] = jnp.concatenate([last, first]).astype(F32).astype(BF)


def get_ids(message_ref):
    ids = message_ref[-2 * IDS :, :].astype(F32)
    return ids[:1], ids[IDS : IDS + 1]


def load_kernel(k_hbm, v_hbm, k_ref, v_ref, sems):
    k_copy = pltpu.make_async_copy(k_hbm, k_ref, sems.at[0])
    v_copy = pltpu.make_async_copy(v_hbm, v_ref, sems.at[1])
    k_copy.start()
    v_copy.start()
    k_copy.wait()
    v_copy.wait()


def split(states, odd, keep_ref, send_ref):
    half = len(states) // 2
    for h in range(half):
        keep_ref[head(h), :] = jnp.where(odd, states[half + h], states[h]).astype(BF)
        send_ref[head(h), :] = jnp.where(odd, states[h], states[half + h]).astype(BF)


def tail_kernel(ids_ref, odd_ref, k_ref, v_ref, keep_ref, send_ref):
    ids = ids_ref[...]
    hit = (column(ids, HEAD) == ids[:, -1:]).astype(F32).astype(BF)
    put_ids(ids, send_ref)
    heads = range(k_ref.shape[1] // HEAD)
    states = [dot(k_ref[:, head(h)] * hit, v_ref[:, head(h)], TN) for h in heads]
    split(states, odd_ref[...] > 0, keep_ref, send_ref)


def chip_kernel(backward, odd_ref, keep_ref, send_ref, theirs_ref, out_ref):
    odd = odd_ref[...] > 0
    mine_kept = ~odd if backward else odd
    which = 1 if backward else 0
    both = get_ids(send_ref)[which] == get_ids(theirs_ref)[which]
    for h in range(keep_ref.shape[0] // HEAD):
        mine, theirs = keep_ref[head(h), :].astype(F32), theirs_ref[head(h), :].astype(F32)
        state = jnp.where(both, mine + theirs, jnp.where(mine_kept, mine, theirs))
        out_ref[head(h), :] = state.astype(BF)
    mine, theirs = send_ref[-2 * IDS :, :].astype(F32), theirs_ref[-2 * IDS :, :].astype(F32)
    out_ref[-2 * IDS :, :] = jnp.where(mine_kept, mine, theirs).astype(BF)


def edge_kernel(odd_ref, keep_ref, send_ref, theirs_ref, near_ref, far_ref, mine_ref, other_ref):
    odd = odd_ref[...] > 0
    ours, others = get_ids(send_ref), get_ids(theirs_ref)
    last_even = jnp.where(odd, others[0], ours[0])
    first_even = jnp.where(odd, others[1], ours[1])
    first_odd = jnp.where(odd, ours[1], others[1])
    take_near, take_far = get_ids(near_ref)[0] == first_even, get_ids(far_ref)[0] == first_even
    take_part = first_odd == last_even
    take_outer = take_part & (last_even == first_even)
    for h in range(keep_ref.shape[0] // HEAD):
        outer = jnp.where(take_near, near_ref[head(h), :].astype(F32), 0.0)
        outer = outer + jnp.where(take_far, far_ref[head(h), :].astype(F32), 0.0)
        part = jnp.where(odd, theirs_ref[head(h), :].astype(F32), keep_ref[head(h), :].astype(F32))
        joined = jnp.where(take_part, part, 0.0) + jnp.where(take_outer, outer, 0.0)
        mine_ref[head(h), :] = jnp.where(odd, joined, outer).astype(BF)
        other_ref[head(h), :] = jnp.where(odd, outer, joined).astype(BF)


def merged(odd_ref, mine_ref, other_ref):
    odd = odd_ref[...] > 0
    half = mine_ref.shape[0] // HEAD

    def state(h):
        mine, other = mine_ref[head(h % half), :].astype(F32), other_ref[head(h % half), :].astype(F32)
        return (jnp.where(odd, other, mine) if h < half else jnp.where(odd, mine, other)).astype(BF)

    return state


def local_kernel(
    ids_ref, q_ref, k_ref, v_ref, g_ref, c_ref, scores_ref, local_ref, up_ref, lead_q_ref, lead_qt_ref
):
    ids = ids_ref[...]
    length = ids.shape[1]
    at = lax.broadcasted_iota(jnp.int32, (length, length), 0)
    of = lax.broadcasted_iota(jnp.int32, (length, length), 1)
    causal = (of <= at) & (column(ids, length) == ids)
    hit = (column(ids, HEAD) == ids[:, :1]).astype(F32)
    for h in range(q_ref.shape[1] // HEAD):
        scores = dot(q_ref[:, head(h)], k_ref[:, head(h)], NT)
        scores = jnp.where(causal, scores, 0.0).astype(BF)
        scores_ref[h] = scores
        local_ref[:, head(h)] = dot(scores, v_ref[:, head(h)], NN)
        gate = jax.nn.sigmoid(g_ref[:, head(h)].astype(F32))
        up_ref[:, head(h)] = c_ref[:, head(h)].astype(F32) * gate
        lead_q = q_ref[:, head(h)].astype(F32) * hit
        lead_q_ref[:, head(h)] = lead_q.astype(BF)
        lead_qt_ref[head(h), :] = lead_q.T.astype(BF)


def attend_kernel(odd_ref, mine_ref, other_ref, lead_q_ref, local_ref, up_ref, before_ref, attended_ref, sums_ref):
    length, states = lead_q_ref.shape
    entering = merged(odd_ref, mine_ref, other_ref)
    square = jnp.zeros((length, HEAD), F32)
    cross = jnp.zeros((length, HEAD), F32)
    for h in range(states // HEAD):
        before = entering(h)
        before_ref[head(h), :] = before
        attended = local_ref[:, head(h)] + dot(lead_q_ref[:, head(h)], before, NN)
        attended_ref[:, head(h)] = attended
        square = square + attended * attended
        cross = cross + up_ref[:, head(h)] * attended
    sums_ref[0:1, :] = jnp.sum(square.T, axis=0, keepdims=True)
    sums_ref[1:2, :] = jnp.sum(cross.T, axis=0, keepdims=True)


def scales(parts):
    total = parts[0][...]
    for part in parts[1:]:
        total = total + part[...]
    inverse = lax.rsqrt(total[0:1, :] / FEATURES + EPSILON)
    factor = inverse * inverse * inverse * total[1:2, :] / FEATURES
    return inverse, factor


def lead_kernel(ids_ref, s0, s1, s2, s3, lead_qt_ref, attended_ref, up_ref, grad_ref, out_ref):
    inverse, factor = scales((s0, s1, s2, s3))
    inverse, factor = column(inverse, HEAD), column(factor, HEAD)
    put_ids(ids_ref[...], out_ref)
    for h in range(up_ref.shape[1] // HEAD):
        grad = up_ref[:, head(h)] * inverse - attended_ref[:, head(h)] * factor
        grad = grad.astype(BF)
        grad_ref[:, head(h)] = grad
        out_ref[head(h), :] = dot(lead_qt_ref[head(h), :], grad, NN).astype(BF)


def back_kernel(
    ids_ref, s0, s1, s2, s3, q_ref, k_ref, v_ref, g_ref, scores_ref, attended_ref, up_ref, grad_ref, before_ref,
    query_grad_ref, gate_grad_ref, key_part_ref, value_part_ref, tail_k_ref, tail_v_ref,
):
    ids = ids_ref[...]
    length = ids.shape[1]
    inverse, _ = scales((s0, s1, s2, s3))
    inverse = column(inverse, HEAD)
    hit = (column(ids, HEAD) == ids[:, :1]).astype(F32).astype(BF)
    tail_hit = (column(ids, HEAD) == ids[:, -1:]).astype(F32).astype(BF)
    at = lax.broadcasted_iota(jnp.int32, (length, length), 0)
    of = lax.broadcasted_iota(jnp.int32, (length, length), 1)
    causal = (of <= at) & (column(ids, length) == ids)
    for h in range(q_ref.shape[1] // HEAD):
        grad = grad_ref[:, head(h)]
        back = jnp.where(causal, dot(grad, v_ref[:, head(h)], NT), 0.0).astype(BF)
        query_grad = dot(back, k_ref[:, head(h)], NN) + dot(grad * hit, before_ref[head(h), :], NT)
        query_grad_ref[:, head(h)] = query_grad.astype(BF)
        key_part_ref[:, head(h)] = dot(back, q_ref[:, head(h)], TN)
        value_part_ref[:, head(h)] = dot(scores_ref[h], grad, TN)
        gate = jax.nn.sigmoid(g_ref[:, head(h)].astype(F32))
        gate_grad = up_ref[:, head(h)] * attended_ref[:, head(h)] * inverse * (1.0 - gate)
        gate_grad_ref[:, head(h)] = gate_grad.astype(BF)
        tail_k_ref[:, head(h)] = k_ref[:, head(h)] * tail_hit
        tail_v_ref[:, head(h)] = v_ref[:, head(h)] * tail_hit


def finish_kernel(
    odd_ref, mine_ref, theirs_ref, came_ref, other_ref, tail_k_ref, tail_v_ref, key_part_ref, value_part_ref,
    key_grad_hbm, value_grad_hbm, key_grad_ref, value_grad_ref, key_sem, value_sem,
):
    odd = odd_ref[...] > 0
    (last, first), (their_last, their_first) = get_ids(mine_ref), get_ids(theirs_ref)
    edge = jnp.where(odd, last, their_last)
    take_came, take_other = get_ids(came_ref)[1] == edge, get_ids(other_ref)[1] == edge
    take_theirs = ~odd & (their_first == last)
    take_outer = odd | (take_theirs & (their_first == their_last))
    copies = []

    def send(ref, hbm, sem, h):
        copies.append(pltpu.make_async_copy(ref.at[:, head(h)], hbm.at[:, head(h)], sem.at[h]))
        copies[-1].start()

    for h in range(tail_k_ref.shape[1] // HEAD):
        outer = jnp.where(take_came, came_ref[head(h), :].astype(F32), 0.0)
        outer = outer + jnp.where(take_other, other_ref[head(h), :].astype(F32), 0.0)
        after = jnp.where(take_theirs, theirs_ref[head(h), :].astype(F32), 0.0)
        after = (after + jnp.where(take_outer, outer, 0.0)).astype(BF)
        key_grad = key_part_ref[:, head(h)] + dot(tail_v_ref[:, head(h)], after, NT)
        key_grad_ref[:, head(h)] = key_grad.astype(BF)
        send(key_grad_ref, key_grad_hbm, key_sem, h)
        value_grad = value_part_ref[:, head(h)] + dot(tail_k_ref[:, head(h)], after, NN)
        value_grad_ref[:, head(h)] = value_grad.astype(BF)
        send(value_grad_ref, value_grad_hbm, value_sem, h)
    for copy in copies:
        copy.wait()


VMEM = pl.BlockSpec(memory_space=pltpu.VMEM)
HBM = pl.BlockSpec(memory_space=pltpu.HBM)


def call(kernel, outs, flops, *args, name=None, in_specs=None, out_specs=None, scratch=(), vmem=24 * MIB):
    size = sum(a.size * a.dtype.itemsize for a in (*args, *outs))
    return pl.pallas_call(
        kernel,
        out_shape=outs,
        in_specs=in_specs or [VMEM] * len(args),
        out_specs=out_specs or [VMEM] * len(outs),
        scratch_shapes=scratch,
        compiler_params=pltpu.CompilerParams(vmem_limit_bytes=vmem),
        cost_estimate=pl.CostEstimate(flops=flops, bytes_accessed=size, transcendentals=0),
        name=name or kernel.__name__,
    )(*args)


def body(queries, keys, values, gates, cotangent, doc_ids):
    length, states = queries.shape
    count, ranks = lax.axis_size("ctx"), lax.axis_size("tp")
    heads = states // HEAD
    shape = jax.ShapeDtypeStruct
    ids = doc_ids.reshape(1, length)
    odd = jnp.broadcast_to(lax.rem(lax.axis_index("ctx"), 2), (1, HEAD))
    half = shape((states // 2, HEAD), BF)
    message = shape((states // 2 + 2 * IDS, HEAD), BF)
    whole = shape((states + 2 * IDS, HEAD), BF)
    wide = shape((length, states), F32)
    narrow = shape((length, states), BF)
    unit = 2 * length * length * states
    buffer, sems = pltpu.VMEM((length, states), BF), pltpu.SemaphoreType.DMA((heads,))

    def swap(x):
        return lax.ppermute(x, "ctx", [(i, i ^ 1) for i in range(count)])

    def shift(x, blocks, wrap=True):
        pairs = [(i, (i + blocks) % count) for i in range(count) if wrap or 0 <= i + blocks < count]
        return lax.ppermute(x, "ctx", pairs)

    def chip(backward, out, *parts):
        name = "chip_lead" if backward else "chip_tail"
        return call(functools.partial(chip_kernel, backward), [out], 0, odd, *parts, name=name)[0]

    keys, values = call(
        load_kernel, [narrow, narrow], 1, keys, values, in_specs=[HBM] * 2, scratch=[pltpu.SemaphoreType.DMA((2,))],
        vmem=52 * MIB + 768 * 1024,
    )
    tail, tail_sent = call(tail_kernel, [half, message], unit // 2, ids, odd, keys, values)
    tail_theirs = swap(tail_sent)
    state = chip(False, message, tail, tail_sent, tail_theirs)
    far = shift(state, 4, False)
    near = shift(state, 2)
    ids, _ = lax.optimization_barrier((ids, state))
    scores, local, up, lead_q, lead_qt = call(
        local_kernel, [shape((heads, length, length), BF), wide, wide, narrow, shape((states, length), BF)], 2 * unit,
        ids, queries, keys, values, gates, cotangent,
    )
    far, near, local = lax.optimization_barrier((far, near, local))
    mine, given = call(edge_kernel, [half, half], 0, odd, tail, tail_sent, tail_theirs, far, near)
    before, attended, sums = call(
        attend_kernel, [shape((states, HEAD), BF), wide, shape((2, length), F32)], unit // 2,
        odd, mine, swap(given), lead_q, local, up,
    )
    parts = [sums] + [lax.ppermute(sums, "tp", [(i, i ^ step) for i in range(ranks)]) for step in (1, 3, 2)]
    grad, lead = call(lead_kernel, [narrow, whole], unit // 2, ids, *parts, lead_qt, attended, up)

    lead_theirs = swap(lead)
    state = chip(True, whole, lead, lead, lead_theirs)
    came = lax.ppermute(state, "ctx", [(i, (i - (2 if i % 2 == 0 else 4)) % count) for i in range(count)])
    ids, _ = lax.optimization_barrier((ids, state))
    query_grad, gate_grad, key_part, value_part, tail_k, tail_v = call(
        back_kernel, [narrow, narrow, wide, wide, narrow, narrow], 5 * unit,
        ids, *parts, queries, keys, values, gates, scores, attended, up, grad, before,
    )
    came, key_part = lax.optimization_barrier((came, key_part))
    key_grad, value_grad = call(
        finish_kernel, [narrow, narrow], unit, odd, lead, lead_theirs, came, swap(came), tail_k, tail_v, key_part, value_part,
        out_specs=[HBM] * 2, scratch=[buffer, buffer, sems, sems],
    )
    return query_grad, key_grad, value_grad, gate_grad


def solution(mesh):
    return jax.shard_map(
        body,
        mesh=mesh,
        in_specs=(P("ctx", "tp"),) * 5 + (P("ctx"),),
        out_specs=(P("ctx", "tp"),) * 4,
        check_vma=False,
    )
```

```python
import functools
import math

import jax
import jax.numpy as jnp
from jax import lax
from jax.experimental import pallas as pl
from jax.experimental.pallas import tpu as pltpu
from jax.sharding import PartitionSpec as P

HEADS = 32
HEAD = 128
EPSILON = 1e-06
FEATURES = HEADS * HEAD
BF = jnp.bfloat16
F32 = jnp.float32
IDS = 8
MIB = 1 << 20


def dot(a, b, dims):
    return lax.dot_general(a, b, (dims, ((), ())), preferred_element_type=F32)


NN = ((1,), (0,))
NT = ((1,), (1,))
TN = ((0,), (0,))


def head(h):
    return slice(h * HEAD, (h + 1) * HEAD)


def column(row, lanes):
    return jnp.broadcast_to(row, (lanes, row.shape[1])).T


def put_ids(ids, out_ref):
    last = jnp.broadcast_to(ids[:, -1:], (IDS, HEAD))
    first = jnp.broadcast_to(ids[:, :1], (IDS, HEAD))
    out_ref[-2 * IDS :, :] = jnp.concatenate([last, first]).astype(F32).astype(BF)


def get_ids(message_ref):
    ids = message_ref[-2 * IDS :, :].astype(F32)
    return ids[:1], ids[IDS : IDS + 1]


def split(states, odd, keep_ref, send_ref):
    half = len(states) // 2
    for h in range(half):
        keep_ref[head(h), :] = jnp.where(odd, states[half + h], states[h]).astype(BF)
        send_ref[head(h), :] = jnp.where(odd, states[h], states[half + h]).astype(BF)


def tail_kernel(ids_hbm, k_hbm, v_hbm, odd_ref, ids_ref, k_ref, v_ref, keep_ref, send_ref, kt_ref, sems):
    loads = ((ids_hbm, ids_ref), (k_hbm, k_ref), (v_hbm, v_ref))
    copies = [pltpu.make_async_copy(hbm, ref, sems.at[i]) for i, (hbm, ref) in enumerate(loads)]
    for copy in copies:
        copy.start()
    heads = range(k_ref.shape[1] // HEAD)
    copies[0].wait()
    ids = ids_ref[...]
    put_ids(ids, send_ref)
    hit = jnp.broadcast_to((ids == ids[:, -1:]).astype(F32).astype(BF), (HEAD, ids.shape[1]))
    copies[1].wait()
    for h in heads:
        kt_ref[head(h), :] = k_ref[:, head(h)].T * hit
    copies[2].wait()
    states = [dot(kt_ref[head(h), :], v_ref[:, head(h)], NN) for h in heads]
    split(states, odd_ref[...] > 0, keep_ref, send_ref)


def chip_kernel(backward, odd_ref, keep_ref, send_ref, theirs_ref, out_ref):
    odd = odd_ref[...] > 0
    mine_kept = ~odd if backward else odd
    which = 1 if backward else 0
    both = get_ids(send_ref)[which] == get_ids(theirs_ref)[which]
    for h in range(keep_ref.shape[0] // HEAD):
        mine, theirs = keep_ref[head(h), :].astype(F32), theirs_ref[head(h), :].astype(F32)
        state = jnp.where(both, mine + theirs, jnp.where(mine_kept, mine, theirs))
        out_ref[head(h), :] = state.astype(BF)
    mine, theirs = send_ref[-2 * IDS :, :].astype(F32), theirs_ref[-2 * IDS :, :].astype(F32)
    out_ref[-2 * IDS :, :] = jnp.where(mine_kept, mine, theirs).astype(BF)


def edge_kernel(odd_ref, keep_ref, send_ref, theirs_ref, near_ref, far_ref, mine_ref, other_ref):
    odd = odd_ref[...] > 0
    ours, others = get_ids(send_ref), get_ids(theirs_ref)
    last_even = jnp.where(odd, others[0], ours[0])
    first_even = jnp.where(odd, others[1], ours[1])
    first_odd = jnp.where(odd, ours[1], others[1])
    take_near, take_far = get_ids(near_ref)[0] == first_even, get_ids(far_ref)[0] == first_even
    take_part = first_odd == last_even
    take_outer = take_part & (last_even == first_even)
    for h in range(keep_ref.shape[0] // HEAD):
        outer = jnp.where(take_near, near_ref[head(h), :].astype(F32), 0.0)
        outer = outer + jnp.where(take_far, far_ref[head(h), :].astype(F32), 0.0)
        part = jnp.where(odd, theirs_ref[head(h), :].astype(F32), keep_ref[head(h), :].astype(F32))
        joined = jnp.where(take_part, part, 0.0) + jnp.where(take_outer, outer, 0.0)
        mine_ref[head(h), :] = jnp.where(odd, joined, outer).astype(BF)
        other_ref[head(h), :] = jnp.where(odd, outer, joined).astype(BF)


def merged(odd_ref, mine_ref, other_ref):
    odd = odd_ref[...] > 0
    half = mine_ref.shape[0] // HEAD

    def state(h):
        mine, other = mine_ref[head(h % half), :].astype(F32), other_ref[head(h % half), :].astype(F32)
        return (jnp.where(odd, other, mine) if h < half else jnp.where(odd, mine, other)).astype(BF)

    return state


def local_kernel(
    ids_ref, q_hbm, k_ref, v_ref, g_hbm, c_hbm, scores_ref, local_ref, up_ref, lead_q_ref, lead_qt_ref,
    q_ref, g_ref, c_ref, sems,
):
    loads = ((q_hbm, q_ref), (g_hbm, g_ref), (c_hbm, c_ref))
    copies = [pltpu.make_async_copy(hbm, ref, sems.at[i]) for i, (hbm, ref) in enumerate(loads)]
    for copy in copies:
        copy.start()
    ids = ids_ref[...]
    length = ids.shape[1]
    at = lax.broadcasted_iota(jnp.int32, (length, length), 0)
    of = lax.broadcasted_iota(jnp.int32, (length, length), 1)
    causal = (of <= at) & (column(ids, length) == ids)
    hit = (column(ids, HEAD) == ids[:, :1]).astype(F32)
    for copy in copies:
        copy.wait()
    for h in range(q_ref.shape[1] // HEAD):
        scores = dot(q_ref[:, head(h)], k_ref[:, head(h)], NT)
        scores = jnp.where(causal, scores, 0.0).astype(BF)
        scores_ref[h] = scores
        local_ref[:, head(h)] = dot(scores, v_ref[:, head(h)], NN)
        gate = jax.nn.sigmoid(g_ref[:, head(h)].astype(F32))
        up_ref[:, head(h)] = c_ref[:, head(h)].astype(F32) * gate
        lead_q = q_ref[:, head(h)].astype(F32) * hit
        lead_q_ref[:, head(h)] = lead_q.astype(BF)
        lead_qt_ref[head(h), :] = lead_q.T.astype(BF)


def attend_kernel(odd_ref, mine_ref, other_ref, lead_q_ref, local_ref, up_ref, before_ref, attended_ref, sums_ref):
    length, states = lead_q_ref.shape
    entering = merged(odd_ref, mine_ref, other_ref)
    square = jnp.zeros((length, HEAD), F32)
    cross = jnp.zeros((length, HEAD), F32)
    for h in range(states // HEAD):
        before = entering(h)
        before_ref[head(h), :] = before
        attended = local_ref[:, head(h)] + dot(lead_q_ref[:, head(h)], before, NN)
        attended_ref[:, head(h)] = attended
        square = square + attended * attended
        cross = cross + up_ref[:, head(h)] * attended
    sums_ref[0:1, :] = jnp.sum(square.T, axis=0, keepdims=True)
    sums_ref[1:2, :] = jnp.sum(cross.T, axis=0, keepdims=True)


def scales(parts):
    total = parts[0][...]
    for part in parts[1:]:
        total = total + part[...]
    inverse = lax.rsqrt(total[0:1, :] / FEATURES + EPSILON)
    factor = inverse * inverse * inverse * total[1:2, :] / FEATURES
    return inverse, factor


def lead_kernel(ids_ref, s0, s1, s2, s3, lead_qt_ref, attended_ref, up_ref, grad_ref, out_ref):
    inverse, factor = scales((s0, s1, s2, s3))
    inverse, factor = column(inverse, HEAD), column(factor, HEAD)
    put_ids(ids_ref[...], out_ref)
    for h in range(up_ref.shape[1] // HEAD):
        grad = up_ref[:, head(h)] * inverse - attended_ref[:, head(h)] * factor
        grad = grad.astype(BF)
        grad_ref[:, head(h)] = grad
        out_ref[head(h), :] = dot(lead_qt_ref[head(h), :], grad, NN).astype(BF)


def back_kernel(
    ids_ref, s0, s1, s2, s3, q_ref, k_ref, v_ref, g_ref, scores_ref, attended_ref, up_ref, grad_ref, before_ref,
    query_grad_ref, gate_grad_ref, key_part_ref, value_part_ref, tail_k_ref, tail_v_ref,
):
    ids = ids_ref[...]
    length = ids.shape[1]
    inverse, _ = scales((s0, s1, s2, s3))
    inverse = column(inverse, HEAD)
    hit = (column(ids, HEAD) == ids[:, :1]).astype(F32).astype(BF)
    tail_hit = (column(ids, HEAD) == ids[:, -1:]).astype(F32).astype(BF)
    at = lax.broadcasted_iota(jnp.int32, (length, length), 0)
    of = lax.broadcasted_iota(jnp.int32, (length, length), 1)
    causal = (of <= at) & (column(ids, length) == ids)
    for h in range(q_ref.shape[1] // HEAD):
        grad = grad_ref[:, head(h)]
        back = jnp.where(causal, dot(grad, v_ref[:, head(h)], NT), 0.0).astype(BF)
        query_grad = dot(back, k_ref[:, head(h)], NN) + dot(grad * hit, before_ref[head(h), :], NT)
        query_grad_ref[:, head(h)] = query_grad.astype(BF)
        key_part_ref[:, head(h)] = dot(back, q_ref[:, head(h)], TN)
        value_part_ref[:, head(h)] = dot(scores_ref[h], grad, TN)
        gate = jax.nn.sigmoid(g_ref[:, head(h)].astype(F32))
        gate_grad = up_ref[:, head(h)] * attended_ref[:, head(h)] * inverse * (1.0 - gate)
        gate_grad_ref[:, head(h)] = gate_grad.astype(BF)
        tail_k_ref[:, head(h)] = k_ref[:, head(h)] * tail_hit
        tail_v_ref[:, head(h)] = v_ref[:, head(h)] * tail_hit


def finish_kernel(
    odd_ref, mine_ref, theirs_ref, came_ref, other_ref, tail_k_ref, tail_v_ref, key_part_ref, value_part_ref,
    key_grad_hbm, value_grad_hbm, key_grad_ref, value_grad_ref, key_sem, value_sem,
):
    odd = odd_ref[...] > 0
    (last, first), (their_last, their_first) = get_ids(mine_ref), get_ids(theirs_ref)
    edge = jnp.where(odd, last, their_last)
    take_came, take_other = get_ids(came_ref)[1] == edge, get_ids(other_ref)[1] == edge
    take_theirs = ~odd & (their_first == last)
    take_outer = odd | (take_theirs & (their_first == their_last))
    copies = []

    def send(ref, hbm, sem, h):
        copies.append(pltpu.make_async_copy(ref.at[:, head(h)], hbm.at[:, head(h)], sem.at[h]))
        copies[-1].start()

    for h in range(tail_k_ref.shape[1] // HEAD):
        outer = jnp.where(take_came, came_ref[head(h), :].astype(F32), 0.0)
        outer = outer + jnp.where(take_other, other_ref[head(h), :].astype(F32), 0.0)
        after = jnp.where(take_theirs, theirs_ref[head(h), :].astype(F32), 0.0)
        after = (after + jnp.where(take_outer, outer, 0.0)).astype(BF)
        key_grad = key_part_ref[:, head(h)] + dot(tail_v_ref[:, head(h)], after, NT)
        key_grad_ref[:, head(h)] = key_grad.astype(BF)
        send(key_grad_ref, key_grad_hbm, key_sem, h)
        value_grad = value_part_ref[:, head(h)] + dot(tail_k_ref[:, head(h)], after, NN)
        value_grad_ref[:, head(h)] = value_grad.astype(BF)
        send(value_grad_ref, value_grad_hbm, value_sem, h)
    for copy in copies:
        copy.wait()


VMEM = pl.BlockSpec(memory_space=pltpu.VMEM)
HBM = pl.BlockSpec(memory_space=pltpu.HBM)


def in_hbm(x):
    return pltpu.with_memory_space_constraint(x, pltpu.HBM)


def call(kernel, outs, flops, *args, name=None, in_specs=None, out_specs=None, scratch=(), vmem=24 * MIB):
    size = sum(math.prod(a.shape) * jnp.dtype(a.dtype).itemsize for a in (*args, *outs))
    return pl.pallas_call(
        kernel,
        out_shape=outs,
        in_specs=in_specs or [VMEM] * len(args),
        out_specs=out_specs or [VMEM] * len(outs),
        scratch_shapes=scratch,
        compiler_params=pltpu.CompilerParams(vmem_limit_bytes=vmem),
        cost_estimate=pl.CostEstimate(flops=flops, bytes_accessed=size, transcendentals=0),
        name=name or kernel.__name__,
    )(*args)


def body(queries, keys, values, gates, cotangent, doc_ids):
    length, states = queries.shape
    count, ranks = lax.axis_size("ctx"), lax.axis_size("tp")
    heads = states // HEAD
    shape = jax.ShapeDtypeStruct
    ids = doc_ids.reshape(1, length)
    odd = jnp.broadcast_to(lax.rem(lax.axis_index("ctx"), 2), (1, HEAD))
    half = shape((states // 2, HEAD), BF)
    message = shape((states // 2 + 2 * IDS, HEAD), BF)
    whole = shape((states + 2 * IDS, HEAD), BF)
    wide = shape((length, states), F32)
    narrow = shape((length, states), BF)
    unit = 2 * length * length * states
    buffer, sems = pltpu.VMEM((length, states), BF), pltpu.SemaphoreType.DMA((heads,))

    def swap(x):
        return lax.ppermute(x, "ctx", [(i, i ^ 1) for i in range(count)])

    def shift(x, blocks, wrap=True):
        pairs = [(i, (i + blocks) % count) for i in range(count) if wrap or 0 <= i + blocks < count]
        return lax.ppermute(x, "ctx", pairs)

    def chip(backward, out, *parts):
        name = "chip_lead" if backward else "chip_tail"
        return call(functools.partial(chip_kernel, backward), [out], 0, odd, *parts, name=name)[0]

    ids, keys, values, tail, tail_sent = call(
        tail_kernel,
        [pltpu.VMEM(ids.shape, ids.dtype)] + [pltpu.VMEM(a.shape, a.dtype) for a in (narrow, narrow, half, message)],
        unit // 2, in_hbm(ids), in_hbm(keys), in_hbm(values), odd,
        in_specs=[HBM] * 3 + [VMEM], scratch=[pltpu.VMEM((states, length), BF), pltpu.SemaphoreType.DMA((3,))],
    )
    tail_theirs = swap(tail_sent)
    state = chip(False, message, tail, tail_sent, tail_theirs)
    far = shift(state, 4, False)
    near = shift(state, 2)
    ids, _ = lax.optimization_barrier((ids, state))
    scores, local, up, lead_q, lead_qt = call(
        local_kernel, [shape((heads, length, length), BF), wide, wide, narrow, shape((states, length), BF)], 2 * unit,
        ids, in_hbm(queries), keys, values, in_hbm(gates), in_hbm(cotangent),
        in_specs=[VMEM, HBM, VMEM, VMEM, HBM, HBM], scratch=[buffer] * 3 + [pltpu.SemaphoreType.DMA((3,))],
    )
    far, near, local = lax.optimization_barrier((far, near, local))
    mine, given = call(edge_kernel, [half, half], 0, odd, tail, tail_sent, tail_theirs, far, near)
    before, attended, sums = call(
        attend_kernel, [shape((states, HEAD), BF), wide, shape((2, length), F32)], unit // 2,
        odd, mine, swap(given), lead_q, local, up,
    )
    parts = [sums] + [lax.ppermute(sums, "tp", [(i, i ^ step) for i in range(ranks)]) for step in (1, 3, 2)]
    grad, lead = call(lead_kernel, [narrow, whole], unit // 2, ids, *parts, lead_qt, attended, up)

    lead_theirs = swap(lead)
    state = chip(True, whole, lead, lead, lead_theirs)
    came = lax.ppermute(state, "ctx", [(i, (i - (2 if i % 2 == 0 else 4)) % count) for i in range(count)])
    ids, _ = lax.optimization_barrier((ids, state))
    query_grad, gate_grad, key_part, value_part, tail_k, tail_v = call(
        back_kernel, [narrow, narrow, wide, wide, narrow, narrow], 5 * unit,
        ids, *parts, queries, keys, values, gates, scores, attended, up, grad, before,
    )
    came, key_part = lax.optimization_barrier((came, key_part))
    key_grad, value_grad = call(
        finish_kernel, [narrow, narrow], unit, odd, lead, lead_theirs, came, swap(came), tail_k, tail_v, key_part, value_part,
        out_specs=[HBM] * 2, scratch=[buffer, buffer, sems, sems],
    )
    return query_grad, key_grad, value_grad, gate_grad


def solution(mesh):
    return jax.shard_map(
        body,
        mesh=mesh,
        in_specs=(P("ctx", "tp"),) * 5 + (P("ctx"),),
        out_specs=(P("ctx", "tp"),) * 4,
        check_vma=False,
    )
```

```python
import functools
import math

import jax
import jax.numpy as jnp
from jax import lax
from jax.experimental import pallas as pl
from jax.experimental.pallas import tpu as pltpu
from jax.sharding import PartitionSpec as P

HEADS = 32
HEAD = 128
EPSILON = 1e-06
FEATURES = HEADS * HEAD
BF = jnp.bfloat16
F32 = jnp.float32
IDS = 8
MIB = 1 << 20


def dot(a, b, dims):
    return lax.dot_general(a, b, (dims, ((), ())), preferred_element_type=F32)


NN = ((1,), (0,))
NT = ((1,), (1,))
TN = ((0,), (0,))


def head(h):
    return slice(h * HEAD, (h + 1) * HEAD)


def column(row, lanes):
    return jnp.broadcast_to(row, (lanes, row.shape[1])).T


def put_ids(ids, out_ref):
    last = jnp.broadcast_to(ids[:, -1:], (IDS, HEAD))
    first = jnp.broadcast_to(ids[:, :1], (IDS, HEAD))
    out_ref[-2 * IDS :, :] = jnp.concatenate([last, first]).astype(F32).astype(BF)


def get_ids(message_ref):
    ids = message_ref[-2 * IDS :, :].astype(F32)
    return ids[:1], ids[IDS : IDS + 1]


def split(states, odd, keep_ref, send_ref):
    half = len(states) // 2
    for h in range(half):
        keep_ref[head(h), :] = jnp.where(odd, states[half + h], states[h]).astype(BF)
        send_ref[head(h), :] = jnp.where(odd, states[h], states[half + h]).astype(BF)


def tail_kernel(ids_hbm, k_hbm, v_hbm, odd_ref, ids_ref, k_ref, v_ref, keep_ref, send_ref, kt_ref, sems):
    loads = ((ids_hbm, ids_ref), (k_hbm, k_ref), (v_hbm, v_ref))
    copies = [pltpu.make_async_copy(hbm, ref, sems.at[i]) for i, (hbm, ref) in enumerate(loads)]
    for copy in copies:
        copy.start()
    heads = range(k_ref.shape[1] // HEAD)
    copies[0].wait()
    ids = ids_ref[...]
    put_ids(ids, send_ref)
    hit = jnp.broadcast_to((ids == ids[:, -1:]).astype(F32).astype(BF), (HEAD, ids.shape[1]))
    copies[1].wait()
    for h in heads:
        kt_ref[head(h), :] = k_ref[:, head(h)].T * hit
    copies[2].wait()
    states = [dot(kt_ref[head(h), :], v_ref[:, head(h)], NN) for h in heads]
    split(states, odd_ref[...] > 0, keep_ref, send_ref)


def chip_kernel(backward, starts, odd_ref, keep_ref, send_ref, theirs_ref, *out_refs):
    odd = odd_ref[...] > 0
    mine_kept = ~odd if backward else odd
    which = 1 if backward else 0
    both = get_ids(send_ref)[which] == get_ids(theirs_ref)[which]
    for h in range(keep_ref.shape[0] // HEAD):
        mine, theirs = keep_ref[head(h), :].astype(F32), theirs_ref[head(h), :].astype(F32)
        state = jnp.where(both, mine + theirs, jnp.where(mine_kept, mine, theirs)).astype(BF)
        for start, ref in zip(starts, out_refs):
            if start <= h < start + ref.shape[0] // HEAD:
                ref[head(h - start), :] = state
    mine, theirs = send_ref[-2 * IDS :, :].astype(F32), theirs_ref[-2 * IDS :, :].astype(F32)
    for ref in out_refs:
        if ref.shape[0] % HEAD:
            ref[-2 * IDS :, :] = jnp.where(mine_kept, mine, theirs).astype(BF)


def edge_kernel(odd_ref, keep_ref, send_ref, theirs_ref, far_rear_ref, far_ref, near_ref, mine_ref, other_ref):
    odd = odd_ref[...] > 0
    ours, others = get_ids(send_ref), get_ids(theirs_ref)
    last_even = jnp.where(odd, others[0], ours[0])
    first_even = jnp.where(odd, others[1], ours[1])
    first_odd = jnp.where(odd, ours[1], others[1])
    take_near, take_far = get_ids(near_ref)[0] == first_even, get_ids(far_ref)[0] == first_even
    take_part = first_odd == last_even
    take_outer = take_part & (last_even == first_even)
    front = far_ref.shape[0] // HEAD
    for h in range(keep_ref.shape[0] // HEAD):
        far = far_ref[head(h), :] if h < front else far_rear_ref[head(h - front), :]
        outer = jnp.where(take_near, near_ref[head(h), :].astype(F32), 0.0)
        outer = outer + jnp.where(take_far, far.astype(F32), 0.0)
        part = jnp.where(odd, theirs_ref[head(h), :].astype(F32), keep_ref[head(h), :].astype(F32))
        joined = jnp.where(take_part, part, 0.0) + jnp.where(take_outer, outer, 0.0)
        mine_ref[head(h), :] = jnp.where(odd, joined, outer).astype(BF)
        other_ref[head(h), :] = jnp.where(odd, outer, joined).astype(BF)


def merged(odd_ref, mine_ref, other_ref):
    odd = odd_ref[...] > 0
    half = mine_ref.shape[0] // HEAD

    def state(h):
        mine, other = mine_ref[head(h % half), :].astype(F32), other_ref[head(h % half), :].astype(F32)
        return (jnp.where(odd, other, mine) if h < half else jnp.where(odd, mine, other)).astype(BF)

    return state


def local_kernel(
    ids_ref, q_hbm, k_ref, v_ref, g_hbm, c_hbm, scores_ref, local_ref, up_ref, lead_q_ref, lead_qt_ref,
    q_ref, g_ref, c_ref, sems,
):
    loads = ((q_hbm, q_ref), (g_hbm, g_ref), (c_hbm, c_ref))
    copies = [pltpu.make_async_copy(hbm, ref, sems.at[i]) for i, (hbm, ref) in enumerate(loads)]
    for copy in copies:
        copy.start()
    ids = ids_ref[...]
    length = ids.shape[1]
    at = lax.broadcasted_iota(jnp.int32, (length, length), 0)
    of = lax.broadcasted_iota(jnp.int32, (length, length), 1)
    causal = (of <= at) & (column(ids, length) == ids)
    hit = (column(ids, HEAD) == ids[:, :1]).astype(F32)
    for copy in copies:
        copy.wait()
    for h in range(q_ref.shape[1] // HEAD):
        scores = dot(q_ref[:, head(h)], k_ref[:, head(h)], NT)
        scores = jnp.where(causal, scores, 0.0).astype(BF)
        scores_ref[h] = scores
        local_ref[:, head(h)] = dot(scores, v_ref[:, head(h)], NN)
        gate = jax.nn.sigmoid(g_ref[:, head(h)].astype(F32))
        up_ref[:, head(h)] = c_ref[:, head(h)].astype(F32) * gate
        lead_q = q_ref[:, head(h)].astype(F32) * hit
        lead_q_ref[:, head(h)] = lead_q.astype(BF)
        lead_qt_ref[head(h), :] = lead_q.T.astype(BF)


def attend_kernel(odd_ref, mine_ref, other_ref, lead_q_ref, local_ref, up_ref, before_ref, attended_ref, sums_ref):
    length, states = lead_q_ref.shape
    entering = merged(odd_ref, mine_ref, other_ref)
    square = jnp.zeros((length, HEAD), F32)
    cross = jnp.zeros((length, HEAD), F32)
    for h in range(states // HEAD):
        before = entering(h)
        before_ref[head(h), :] = before
        attended = local_ref[:, head(h)] + dot(lead_q_ref[:, head(h)], before, NN)
        attended_ref[:, head(h)] = attended
        square = square + attended * attended
        cross = cross + up_ref[:, head(h)] * attended
    sums_ref[0:1, :] = jnp.sum(square.T, axis=0, keepdims=True)
    sums_ref[1:2, :] = jnp.sum(cross.T, axis=0, keepdims=True)


def scales(parts):
    total = parts[0][...]
    for part in parts[1:]:
        total = total + part[...]
    inverse = lax.rsqrt(total[0:1, :] / FEATURES + EPSILON)
    factor = inverse * inverse * inverse * total[1:2, :] / FEATURES
    return inverse, factor


def lead_kernel(ids_ref, s0, s1, s2, s3, lead_qt_ref, attended_ref, up_ref, grad_ref, out_ref):
    inverse, factor = scales((s0, s1, s2, s3))
    inverse, factor = column(inverse, HEAD), column(factor, HEAD)
    put_ids(ids_ref[...], out_ref)
    for h in range(up_ref.shape[1] // HEAD):
        grad = up_ref[:, head(h)] * inverse - attended_ref[:, head(h)] * factor
        grad = grad.astype(BF)
        grad_ref[:, head(h)] = grad
        out_ref[head(h), :] = dot(lead_qt_ref[head(h), :], grad, NN).astype(BF)


def back_kernel(
    ids_ref, s0, s1, s2, s3, q_ref, k_ref, v_ref, g_ref, scores_ref, attended_ref, up_ref, grad_ref, before_ref,
    query_grad_ref, gate_grad_ref, key_part_ref, value_part_ref, tail_k_ref, tail_v_ref,
):
    ids = ids_ref[...]
    length = ids.shape[1]
    inverse, _ = scales((s0, s1, s2, s3))
    inverse = column(inverse, HEAD)
    hit = (column(ids, HEAD) == ids[:, :1]).astype(F32).astype(BF)
    tail_hit = (column(ids, HEAD) == ids[:, -1:]).astype(F32).astype(BF)
    at = lax.broadcasted_iota(jnp.int32, (length, length), 0)
    of = lax.broadcasted_iota(jnp.int32, (length, length), 1)
    causal = (of <= at) & (column(ids, length) == ids)
    for h in range(q_ref.shape[1] // HEAD):
        grad = grad_ref[:, head(h)]
        back = jnp.where(causal, dot(grad, v_ref[:, head(h)], NT), 0.0).astype(BF)
        query_grad = dot(back, k_ref[:, head(h)], NN) + dot(grad * hit, before_ref[head(h), :], NT)
        query_grad_ref[:, head(h)] = query_grad.astype(BF)
        key_part_ref[:, head(h)] = dot(back, q_ref[:, head(h)], TN)
        value_part_ref[:, head(h)] = dot(scores_ref[h], grad, TN)
        gate = jax.nn.sigmoid(g_ref[:, head(h)].astype(F32))
        gate_grad = up_ref[:, head(h)] * attended_ref[:, head(h)] * inverse * (1.0 - gate)
        gate_grad_ref[:, head(h)] = gate_grad.astype(BF)
        tail_k_ref[:, head(h)] = k_ref[:, head(h)] * tail_hit
        tail_v_ref[:, head(h)] = v_ref[:, head(h)] * tail_hit


def finish_kernel(
    odd_ref, mine_ref, theirs_ref, front_ref, front_other_ref, rear_ref, rear_other_ref, tail_k_ref, tail_v_ref,
    key_part_ref, value_part_ref, key_grad_hbm, value_grad_hbm, key_grad_ref, value_grad_ref, key_sem, value_sem,
):
    odd = odd_ref[...] > 0
    (last, first), (their_last, their_first) = get_ids(mine_ref), get_ids(theirs_ref)
    edge = jnp.where(odd, last, their_last)
    take_came, take_other = get_ids(front_ref)[1] == edge, get_ids(front_other_ref)[1] == edge
    take_theirs = ~odd & (their_first == last)
    take_outer = odd | (take_theirs & (their_first == their_last))
    came = [(front_ref, front_other_ref, h) for h in range(front_ref.shape[0] // HEAD)]
    came += [(rear_ref, rear_other_ref, h) for h in range(rear_ref.shape[0] // HEAD)]
    copies = []

    def send(ref, hbm, sem, h):
        copies.append(pltpu.make_async_copy(ref.at[:, head(h)], hbm.at[:, head(h)], sem.at[h]))
        copies[-1].start()

    for h, (came_ref, other_ref, at) in enumerate(came):
        outer = jnp.where(take_came, came_ref[head(at), :].astype(F32), 0.0)
        outer = outer + jnp.where(take_other, other_ref[head(at), :].astype(F32), 0.0)
        after = jnp.where(take_theirs, theirs_ref[head(h), :].astype(F32), 0.0)
        after = (after + jnp.where(take_outer, outer, 0.0)).astype(BF)
        key_grad = key_part_ref[:, head(h)] + dot(tail_v_ref[:, head(h)], after, NT)
        key_grad_ref[:, head(h)] = key_grad.astype(BF)
        send(key_grad_ref, key_grad_hbm, key_sem, h)
        value_grad = value_part_ref[:, head(h)] + dot(tail_k_ref[:, head(h)], after, NN)
        value_grad_ref[:, head(h)] = value_grad.astype(BF)
        send(value_grad_ref, value_grad_hbm, value_sem, h)
    for copy in copies:
        copy.wait()


VMEM = pl.BlockSpec(memory_space=pltpu.VMEM)
HBM = pl.BlockSpec(memory_space=pltpu.HBM)


def in_hbm(x):
    return pltpu.with_memory_space_constraint(x, pltpu.HBM)


def call(kernel, outs, flops, *args, name=None, in_specs=None, out_specs=None, scratch=()):
    size = sum(math.prod(a.shape) * jnp.dtype(a.dtype).itemsize for a in (*args, *outs))
    return pl.pallas_call(
        kernel,
        out_shape=outs,
        in_specs=in_specs or [VMEM] * len(args),
        out_specs=out_specs or [VMEM] * len(outs),
        scratch_shapes=scratch,
        compiler_params=pltpu.CompilerParams(vmem_limit_bytes=24 * MIB),
        cost_estimate=pl.CostEstimate(flops=flops, bytes_accessed=size, transcendentals=0),
        name=name or kernel.__name__,
    )(*args)


def body(queries, keys, values, gates, cotangent, doc_ids):
    length, states = queries.shape
    count, ranks = lax.axis_size("ctx"), lax.axis_size("tp")
    heads = states // HEAD
    shape = jax.ShapeDtypeStruct
    ids = doc_ids.reshape(1, length)
    odd = jnp.broadcast_to(lax.rem(lax.axis_index("ctx"), 2), (1, HEAD))
    half = shape((states // 2, HEAD), BF)
    message = shape((states // 2 + 2 * IDS, HEAD), BF)
    whole = shape((states + 2 * IDS, HEAD), BF)
    wide = shape((length, states), F32)
    narrow = shape((length, states), BF)
    unit = 2 * length * length * states
    buffer, sems = pltpu.VMEM((length, states), BF), pltpu.SemaphoreType.DMA((heads,))

    def swap(x):
        return lax.ppermute(x, "ctx", [(i, i ^ 1) for i in range(count)])

    def shift(x, blocks, wrap=True):
        pairs = [(i, (i + blocks) % count) for i in range(count) if wrap or 0 <= i + blocks < count]
        return lax.ppermute(x, "ctx", pairs)

    def chip(backward, starts, outs, *parts):
        name = "chip_lead" if backward else "chip_tail"
        return call(functools.partial(chip_kernel, backward, starts), outs, 0, odd, *parts, name=name)

    ids, keys, values, tail, tail_sent = call(
        tail_kernel,
        [pltpu.VMEM(ids.shape, ids.dtype)] + [pltpu.VMEM(a.shape, a.dtype) for a in (narrow, narrow, half, message)],
        unit // 2, in_hbm(ids), in_hbm(keys), in_hbm(values), odd,
        in_specs=[HBM] * 3 + [VMEM], scratch=[pltpu.VMEM((states, length), BF), pltpu.SemaphoreType.DMA((3,))],
    )
    tail_theirs = swap(tail_sent)
    outs = [message, shape((2 * HEAD + 2 * IDS, HEAD), BF), shape(((heads // 2 - 2) * HEAD, HEAD), BF)]
    state, front, rear = chip(False, (0, 0, 2), outs, tail, tail_sent, tail_theirs)
    near, far, far_rear = shift(state, 2), shift(front, 4), shift(rear, 4, False)
    ids, _ = lax.optimization_barrier((ids, state))
    scores, local, up, lead_q, lead_qt = call(
        local_kernel, [shape((heads, length, length), BF), wide, wide, narrow, shape((states, length), BF)], 2 * unit,
        ids, in_hbm(queries), keys, values, in_hbm(gates), in_hbm(cotangent),
        in_specs=[VMEM, HBM, VMEM, VMEM, HBM, HBM], scratch=[buffer] * 3 + [pltpu.SemaphoreType.DMA((3,))],
    )
    far_rear, far, near, local = lax.optimization_barrier((far_rear, far, near, local))
    mine, given = call(edge_kernel, [half, half], 0, odd, tail, tail_sent, tail_theirs, far_rear, far, near)
    before, attended, sums = call(
        attend_kernel, [shape((states, HEAD), BF), wide, shape((2, length), F32)], unit // 2,
        odd, mine, swap(given), lead_q, local, up,
    )
    parts = [sums] + [lax.ppermute(sums, "tp", [(i, i ^ step) for i in range(ranks)]) for step in (1, 3, 2)]
    grad, lead = call(lead_kernel, [narrow, whole], unit // 2, ids, *parts, lead_qt, attended, up)

    def spread(x, wrap):
        pairs = [(i, i - (2 if i % 2 == 0 else 4)) for i in range(count)]
        return lax.ppermute(x, "ctx", [(i, j % count) for i, j in pairs if wrap or j >= 0])

    lead_theirs = swap(lead)
    cut = 6 * heads // 8
    outs = [shape((cut * HEAD + 2 * IDS, HEAD), BF), shape(((heads - cut) * HEAD, HEAD), BF)]
    front, rear = chip(True, (0, cut), outs, lead, lead, lead_theirs)
    front_came, rear_came = spread(front, True), spread(rear, False)
    ids, _ = lax.optimization_barrier((ids, front))
    query_grad, gate_grad, key_part, value_part, tail_k, tail_v = call(
        back_kernel, [narrow, narrow, wide, wide, narrow, narrow], 5 * unit,
        ids, *parts, queries, keys, values, gates, scores, attended, up, grad, before,
    )
    rear_came, front_came, key_part = lax.optimization_barrier((rear_came, front_came, key_part))
    key_grad, value_grad = call(
        finish_kernel, [narrow, narrow], unit, odd, lead, lead_theirs, front_came, swap(front_came), rear_came,
        swap(rear_came), tail_k, tail_v, key_part, value_part, out_specs=[HBM] * 2, scratch=[buffer, buffer, sems, sems],
    )
    return query_grad, key_grad, value_grad, gate_grad


def solution(mesh):
    return jax.shard_map(
        body,
        mesh=mesh,
        in_specs=(P("ctx", "tp"),) * 5 + (P("ctx"),),
        out_specs=(P("ctx", "tp"),) * 4,
        check_vma=False,
    )
```

```python
import functools
import math

import jax
import jax.numpy as jnp
from jax import lax
from jax.experimental import pallas as pl
from jax.experimental.pallas import tpu as pltpu
from jax.sharding import PartitionSpec as P

HEADS = 32
HEAD = 128
EPSILON = 1e-06
FEATURES = HEADS * HEAD
BF = jnp.bfloat16
F32 = jnp.float32
IDS = 8
MIB = 1 << 20


def dot(a, b, dims):
    return lax.dot_general(a, b, (dims, ((), ())), preferred_element_type=F32)


NN = ((1,), (0,))
NT = ((1,), (1,))
TN = ((0,), (0,))


def head(h):
    return slice(h * HEAD, (h + 1) * HEAD)


def column(row, lanes):
    return jnp.broadcast_to(row, (lanes, row.shape[1])).T


def put_ids(ids, out_ref):
    last = jnp.broadcast_to(ids[:, -1:], (IDS, HEAD))
    first = jnp.broadcast_to(ids[:, :1], (IDS, HEAD))
    out_ref[-2 * IDS :, :] = jnp.concatenate([last, first]).astype(F32).astype(BF)


def get_ids(message_ref):
    ids = message_ref[-2 * IDS :, :].astype(F32)
    return ids[:1], ids[IDS : IDS + 1]


def split(states, odd, keep_ref, send_ref):
    half = len(states) // 2
    for h in range(half):
        keep_ref[head(h), :] = jnp.where(odd, states[half + h], states[h]).astype(BF)
        send_ref[head(h), :] = jnp.where(odd, states[h], states[half + h]).astype(BF)


def tail_kernel(ids_hbm, k_hbm, v_hbm, odd_ref, ids_ref, k_ref, v_ref, keep_ref, send_ref, kt_ref, sems):
    loads = ((ids_hbm, ids_ref), (k_hbm, k_ref), (v_hbm, v_ref))
    copies = [pltpu.make_async_copy(hbm, ref, sems.at[i]) for i, (hbm, ref) in enumerate(loads)]
    for copy in copies:
        copy.start()
    heads = range(k_ref.shape[1] // HEAD)
    copies[0].wait()
    ids = ids_ref[...]
    put_ids(ids, send_ref)
    hit = jnp.broadcast_to((ids == ids[:, -1:]).astype(F32).astype(BF), (HEAD, ids.shape[1]))
    copies[1].wait()
    for h in heads:
        kt_ref[head(h), :] = k_ref[:, head(h)].T * hit
    copies[2].wait()
    states = [dot(kt_ref[head(h), :], v_ref[:, head(h)], NN) for h in heads]
    split(states, odd_ref[...] > 0, keep_ref, send_ref)


def chip_kernel(backward, starts, odd_ref, keep_ref, send_ref, theirs_ref, *out_refs):
    odd = odd_ref[...] > 0
    mine_kept = ~odd if backward else odd
    which = 1 if backward else 0
    both = get_ids(send_ref)[which] == get_ids(theirs_ref)[which]
    for h in range(keep_ref.shape[0] // HEAD):
        mine, theirs = keep_ref[head(h), :].astype(F32), theirs_ref[head(h), :].astype(F32)
        state = jnp.where(both, mine + theirs, jnp.where(mine_kept, mine, theirs)).astype(BF)
        for start, ref in zip(starts, out_refs):
            if start <= h < start + ref.shape[0] // HEAD:
                ref[head(h - start), :] = state
    mine, theirs = send_ref[-2 * IDS :, :].astype(F32), theirs_ref[-2 * IDS :, :].astype(F32)
    for ref in out_refs:
        if ref.shape[0] % HEAD:
            ref[-2 * IDS :, :] = jnp.where(mine_kept, mine, theirs).astype(BF)


def edge_kernel(odd_ref, keep_ref, send_ref, theirs_ref, far_rear_ref, far_ref, near_ref, mine_ref, other_ref):
    odd = odd_ref[...] > 0
    ours, others = get_ids(send_ref), get_ids(theirs_ref)
    last_even = jnp.where(odd, others[0], ours[0])
    first_even = jnp.where(odd, others[1], ours[1])
    first_odd = jnp.where(odd, ours[1], others[1])
    take_near, take_far = get_ids(near_ref)[0] == first_even, get_ids(far_ref)[0] == first_even
    take_part = first_odd == last_even
    take_outer = take_part & (last_even == first_even)
    front = far_ref.shape[0] // HEAD
    for h in range(keep_ref.shape[0] // HEAD):
        far = far_ref[head(h), :] if h < front else far_rear_ref[head(h - front), :]
        outer = jnp.where(take_near, near_ref[head(h), :].astype(F32), 0.0)
        outer = outer + jnp.where(take_far, far.astype(F32), 0.0)
        part = jnp.where(odd, theirs_ref[head(h), :].astype(F32), keep_ref[head(h), :].astype(F32))
        joined = jnp.where(take_part, part, 0.0) + jnp.where(take_outer, outer, 0.0)
        mine_ref[head(h), :] = jnp.where(odd, joined, outer).astype(BF)
        other_ref[head(h), :] = jnp.where(odd, outer, joined).astype(BF)


def merged(odd_ref, mine_ref, other_ref):
    odd = odd_ref[...] > 0
    half = mine_ref.shape[0] // HEAD

    def state(h):
        mine, other = mine_ref[head(h % half), :].astype(F32), other_ref[head(h % half), :].astype(F32)
        return (jnp.where(odd, other, mine) if h < half else jnp.where(odd, mine, other)).astype(BF)

    return state


def local_kernel(
    ids_ref, q_hbm, k_ref, v_ref, g_hbm, c_hbm, scores_ref, local_ref, up_ref, lead_q_ref, lead_qt_ref,
    q_ref, g_ref, c_ref, sems,
):
    loads = ((q_hbm, q_ref), (g_hbm, g_ref), (c_hbm, c_ref))
    copies = [pltpu.make_async_copy(hbm, ref, sems.at[i]) for i, (hbm, ref) in enumerate(loads)]
    for copy in copies:
        copy.start()
    ids = ids_ref[...]
    length = ids.shape[1]
    at = lax.broadcasted_iota(jnp.int32, (length, length), 0)
    of = lax.broadcasted_iota(jnp.int32, (length, length), 1)
    causal = (of <= at) & (column(ids, length) == ids)
    hit = (column(ids, HEAD) == ids[:, :1]).astype(F32)
    for copy in copies:
        copy.wait()
    for h in range(q_ref.shape[1] // HEAD):
        scores = dot(q_ref[:, head(h)], k_ref[:, head(h)], NT)
        scores = jnp.where(causal, scores, 0.0).astype(BF)
        scores_ref[h] = scores
        local_ref[:, head(h)] = dot(scores, v_ref[:, head(h)], NN)
        gate = jax.nn.sigmoid(g_ref[:, head(h)].astype(F32))
        up_ref[:, head(h)] = c_ref[:, head(h)].astype(F32) * gate
        lead_q = q_ref[:, head(h)].astype(F32) * hit
        lead_q_ref[:, head(h)] = lead_q.astype(BF)
        lead_qt_ref[head(h), :] = lead_q.T.astype(BF)


def attend_kernel(odd_ref, mine_ref, other_ref, lead_q_ref, local_ref, up_ref, before_ref, attended_ref, sums_ref):
    length, states = lead_q_ref.shape
    entering = merged(odd_ref, mine_ref, other_ref)
    square = jnp.zeros((length, HEAD), F32)
    cross = jnp.zeros((length, HEAD), F32)
    for h in range(states // HEAD):
        before = entering(h)
        before_ref[head(h), :] = before
        attended = local_ref[:, head(h)] + dot(lead_q_ref[:, head(h)], before, NN)
        attended_ref[:, head(h)] = attended
        square = square + attended * attended
        cross = cross + up_ref[:, head(h)] * attended
    sums_ref[0:1, :] = jnp.sum(square.T, axis=0, keepdims=True)
    sums_ref[1:2, :] = jnp.sum(cross.T, axis=0, keepdims=True)


def scales(parts):
    total = parts[0][...]
    for part in parts[1:]:
        total = total + part[...]
    inverse = lax.rsqrt(total[0:1, :] / FEATURES + EPSILON)
    factor = inverse * inverse * inverse * total[1:2, :] / FEATURES
    return inverse, factor


def lead_kernel(ids_ref, s0, s1, s2, s3, lead_qt_ref, attended_ref, up_ref, grad_ref, out_ref):
    inverse, factor = scales((s0, s1, s2, s3))
    inverse, factor = column(inverse, HEAD), column(factor, HEAD)
    put_ids(ids_ref[...], out_ref)
    for h in range(up_ref.shape[1] // HEAD):
        grad = up_ref[:, head(h)] * inverse - attended_ref[:, head(h)] * factor
        grad = grad.astype(BF)
        grad_ref[:, head(h)] = grad
        out_ref[head(h), :] = dot(lead_qt_ref[head(h), :], grad, NN).astype(BF)


def back_kernel(
    ids_ref, s0, s1, s2, s3, q_ref, k_ref, v_ref, g_ref, scores_ref, attended_ref, up_ref, grad_ref, before_ref,
    query_grad_ref, gate_grad_ref, key_part_ref, value_part_ref, tail_k_ref, tail_v_ref,
):
    ids = ids_ref[...]
    length = ids.shape[1]
    inverse, _ = scales((s0, s1, s2, s3))
    inverse = column(inverse, HEAD)
    hit = (column(ids, HEAD) == ids[:, :1]).astype(F32).astype(BF)
    tail_hit = (column(ids, HEAD) == ids[:, -1:]).astype(F32).astype(BF)
    at = lax.broadcasted_iota(jnp.int32, (length, length), 0)
    of = lax.broadcasted_iota(jnp.int32, (length, length), 1)
    causal = (of <= at) & (column(ids, length) == ids)
    for h in range(q_ref.shape[1] // HEAD):
        grad = grad_ref[:, head(h)]
        back = jnp.where(causal, dot(grad, v_ref[:, head(h)], NT), 0.0).astype(BF)
        query_grad = dot(back, k_ref[:, head(h)], NN) + dot(grad * hit, before_ref[head(h), :], NT)
        query_grad_ref[:, head(h)] = query_grad.astype(BF)
        key_part_ref[:, head(h)] = dot(back, q_ref[:, head(h)], TN)
        value_part_ref[:, head(h)] = dot(scores_ref[h], grad, TN)
        gate = jax.nn.sigmoid(g_ref[:, head(h)].astype(F32))
        gate_grad = up_ref[:, head(h)] * attended_ref[:, head(h)] * inverse * (1.0 - gate)
        gate_grad_ref[:, head(h)] = gate_grad.astype(BF)
        tail_k_ref[:, head(h)] = k_ref[:, head(h)] * tail_hit
        tail_v_ref[:, head(h)] = v_ref[:, head(h)] * tail_hit


def finish_kernel(
    odd_ref, mine_ref, theirs_ref, front_ref, front_other_ref, rear_ref, rear_other_ref, tail_k_ref, tail_v_ref,
    key_part_ref, value_part_ref, key_grad_hbm, value_grad_hbm, key_grad_ref, value_grad_ref, key_sem, value_sem,
):
    odd = odd_ref[...] > 0
    (last, first), (their_last, their_first) = get_ids(mine_ref), get_ids(theirs_ref)
    edge = jnp.where(odd, last, their_last)
    take_came, take_other = get_ids(front_ref)[1] == edge, get_ids(front_other_ref)[1] == edge
    take_theirs = ~odd & (their_first == last)
    take_outer = odd | (take_theirs & (their_first == their_last))
    came = [(front_ref, front_other_ref, h) for h in range(front_ref.shape[0] // HEAD)]
    came += [(rear_ref, rear_other_ref, h) for h in range(rear_ref.shape[0] // HEAD)]
    copies = []

    def send(ref, hbm, sem, h):
        copies.append(pltpu.make_async_copy(ref.at[:, head(h)], hbm.at[:, head(h)], sem.at[h]))
        copies[-1].start()

    for h, (came_ref, other_ref, at) in enumerate(came):
        outer = jnp.where(take_came, came_ref[head(at), :].astype(F32), 0.0)
        outer = outer + jnp.where(take_other, other_ref[head(at), :].astype(F32), 0.0)
        after = jnp.where(take_theirs, theirs_ref[head(h), :].astype(F32), 0.0)
        after = (after + jnp.where(take_outer, outer, 0.0)).astype(BF)
        key_grad = key_part_ref[:, head(h)] + dot(tail_v_ref[:, head(h)], after, NT)
        key_grad_ref[:, head(h)] = key_grad.astype(BF)
        send(key_grad_ref, key_grad_hbm, key_sem, h)
        value_grad = value_part_ref[:, head(h)] + dot(tail_k_ref[:, head(h)], after, NN)
        value_grad_ref[:, head(h)] = value_grad.astype(BF)
        send(value_grad_ref, value_grad_hbm, value_sem, h)
    for copy in copies:
        copy.wait()


VMEM = pl.BlockSpec(memory_space=pltpu.VMEM)
HBM = pl.BlockSpec(memory_space=pltpu.HBM)


def in_hbm(x):
    return pltpu.with_memory_space_constraint(x, pltpu.HBM)


def call(kernel, outs, flops, *args, name=None, in_specs=None, out_specs=None, scratch=()):
    size = sum(math.prod(a.shape) * jnp.dtype(a.dtype).itemsize for a in (*args, *outs))
    return pl.pallas_call(
        kernel,
        out_shape=outs,
        in_specs=in_specs or [VMEM] * len(args),
        out_specs=out_specs or [VMEM] * len(outs),
        scratch_shapes=scratch,
        compiler_params=pltpu.CompilerParams(vmem_limit_bytes=24 * MIB),
        cost_estimate=pl.CostEstimate(flops=flops, bytes_accessed=size, transcendentals=0),
        name=name or kernel.__name__,
    )(*args)


def body(queries, keys, values, gates, cotangent, doc_ids):
    length, states = queries.shape
    count, ranks = lax.axis_size("ctx"), lax.axis_size("tp")
    heads = states // HEAD
    shape = jax.ShapeDtypeStruct
    ids = doc_ids.reshape(1, length)
    odd = jnp.broadcast_to(lax.rem(lax.axis_index("ctx"), 2), (1, HEAD))
    half = shape((states // 2, HEAD), BF)
    message = shape((states // 2 + 2 * IDS, HEAD), BF)
    whole = shape((states + 2 * IDS, HEAD), BF)
    wide = shape((length, states), F32)
    narrow = shape((length, states), BF)
    unit = 2 * length * length * states
    buffer, sems = pltpu.VMEM((length, states), BF), pltpu.SemaphoreType.DMA((heads,))

    def swap(x):
        return lax.ppermute(x, "ctx", [(i, i ^ 1) for i in range(count)])

    def shift(x, blocks, wrap=True):
        pairs = [(i, (i + blocks) % count) for i in range(count) if wrap or 0 <= i + blocks < count]
        return lax.ppermute(x, "ctx", pairs)

    def chip(backward, starts, outs, *parts):
        name = "chip_lead" if backward else "chip_tail"
        return call(functools.partial(chip_kernel, backward, starts), outs, 0, odd, *parts, name=name)

    ids, keys, values, tail, tail_sent = call(
        tail_kernel,
        [pltpu.VMEM(ids.shape, ids.dtype)] + [pltpu.VMEM(a.shape, a.dtype) for a in (narrow, narrow, half, message)],
        unit // 2, in_hbm(ids), in_hbm(keys), in_hbm(values), odd,
        in_specs=[HBM] * 3 + [VMEM], scratch=[pltpu.VMEM((states, length), BF), pltpu.SemaphoreType.DMA((3,))],
    )
    tail_theirs = swap(tail_sent)
    outs = [message, shape((2 * HEAD + 2 * IDS, HEAD), BF), shape(((heads // 2 - 2) * HEAD, HEAD), BF)]
    state, front, rear = chip(False, (0, 0, 2), outs, tail, tail_sent, tail_theirs)
    near, far, far_rear = shift(state, 2), shift(front, 4), shift(rear, 4, False)
    ids, _ = lax.optimization_barrier((ids, state))
    scores, local, up, lead_q, lead_qt = call(
        local_kernel, [shape((heads, length, length), BF), wide, wide, narrow, shape((states, length), BF)], 2 * unit,
        ids, in_hbm(queries), keys, values, in_hbm(gates), in_hbm(cotangent),
        in_specs=[VMEM, HBM, VMEM, VMEM, HBM, HBM], scratch=[buffer] * 3 + [pltpu.SemaphoreType.DMA((3,))],
    )
    far_rear, far, near, local = lax.optimization_barrier((far_rear, far, near, local))
    mine, given = call(edge_kernel, [half, half], 0, odd, tail, tail_sent, tail_theirs, far_rear, far, near)
    before, attended, sums = call(
        attend_kernel, [shape((states, HEAD), BF), wide, shape((2, length), F32)], unit // 2,
        odd, mine, swap(given), lead_q, local, up,
    )
    parts = [sums] + [lax.ppermute(sums, "tp", [(i, i ^ step) for i in range(ranks)]) for step in (1, 3, 2)]
    grad, lead = call(lead_kernel, [narrow, whole], unit // 2, ids, *parts, lead_qt, attended, up)

    def spread(x, wrap):
        pairs = [(i, i - (2 if i % 2 == 0 else 4)) for i in range(count)]
        useful = [(i, j) for i, j in pairs if j >= 0]
        spare = [(0, count - 3), (1, count - 2), (3, count - 1)] if wrap else []
        return lax.ppermute(x, "ctx", useful + spare)

    lead_theirs = swap(lead)
    cut = 6 * heads // 8
    outs = [shape((cut * HEAD + 2 * IDS, HEAD), BF), shape(((heads - cut) * HEAD, HEAD), BF)]
    front, rear = chip(True, (0, cut), outs, lead, lead, lead_theirs)
    front_came, rear_came = spread(front, True), spread(rear, False)
    ids, _ = lax.optimization_barrier((ids, front))
    query_grad, gate_grad, key_part, value_part, tail_k, tail_v = call(
        back_kernel, [narrow, narrow, wide, wide, narrow, narrow], 5 * unit,
        ids, *parts, queries, keys, values, gates, scores, attended, up, grad, before,
    )
    rear_came, front_came, key_part = lax.optimization_barrier((rear_came, front_came, key_part))
    key_grad, value_grad = call(
        finish_kernel, [narrow, narrow], unit, odd, lead, lead_theirs, front_came, swap(front_came), rear_came,
        swap(rear_came), tail_k, tail_v, key_part, value_part, out_specs=[HBM] * 2, scratch=[buffer, buffer, sems, sems],
    )
    return query_grad, key_grad, value_grad, gate_grad


def solution(mesh):
    return jax.shard_map(
        body,
        mesh=mesh,
        in_specs=(P("ctx", "tp"),) * 5 + (P("ctx"),),
        out_specs=(P("ctx", "tp"),) * 4,
        check_vma=False,
    )
```

```python
import functools
import math

import jax
import jax.numpy as jnp
from jax import lax
from jax.experimental import pallas as pl
from jax.experimental.pallas import tpu as pltpu
from jax.sharding import PartitionSpec as P

HEADS = 32
HEAD = 128
EPSILON = 1e-06
FEATURES = HEADS * HEAD
BF = jnp.bfloat16
F32 = jnp.float32
IDS = 8
MIB = 1 << 20


def dot(a, b, dims):
    return lax.dot_general(a, b, (dims, ((), ())), preferred_element_type=F32)


NN = ((1,), (0,))
NT = ((1,), (1,))
TN = ((0,), (0,))


def head(h):
    return slice(h * HEAD, (h + 1) * HEAD)


def column(row, lanes):
    return jnp.broadcast_to(row, (lanes, row.shape[1])).T


def put_ids(ids, out_ref):
    last = jnp.broadcast_to(ids[:, -1:], (IDS, HEAD))
    first = jnp.broadcast_to(ids[:, :1], (IDS, HEAD))
    out_ref[-2 * IDS :, :] = jnp.concatenate([last, first]).astype(F32).astype(BF)


def get_ids(message_ref):
    ids = message_ref[-2 * IDS :, :].astype(F32)
    return ids[:1], ids[IDS : IDS + 1]


def split(states, odd, keep_ref, send_ref):
    half = len(states) // 2
    for h in range(half):
        keep_ref[head(h), :] = jnp.where(odd, states[half + h], states[h]).astype(BF)
        send_ref[head(h), :] = jnp.where(odd, states[h], states[half + h]).astype(BF)


def tail_kernel(ids_hbm, k_hbm, v_hbm, odd_ref, ids_ref, k_ref, v_ref, keep_ref, send_ref, kt_ref, sems):
    rows = k_ref.shape[0] // 2
    parts = [slice(p * rows, (p + 1) * rows) for p in range(2)]
    loads = [(ids_hbm, ids_ref)] + [(k_hbm.at[part], k_ref.at[part]) for part in parts] + [(v_hbm, v_ref)]
    copies = [pltpu.make_async_copy(hbm, ref, sems.at[i]) for i, (hbm, ref) in enumerate(loads)]
    for copy in copies:
        copy.start()
    heads = range(k_ref.shape[1] // HEAD)
    copies[0].wait()
    ids = ids_ref[...]
    put_ids(ids, send_ref)
    hit = jnp.broadcast_to((ids == ids[:, -1:]).astype(F32).astype(BF), (HEAD, ids.shape[1]))
    for part, copy in zip(parts, copies[1:3]):
        copy.wait()
        for h in heads:
            kt_ref[head(h), part] = k_ref[part, head(h)].T * hit[:, part]
    copies[3].wait()
    states = [dot(kt_ref[head(h), :], v_ref[:, head(h)], NN) for h in heads]
    split(states, odd_ref[...] > 0, keep_ref, send_ref)


def chip_kernel(backward, starts, odd_ref, keep_ref, send_ref, theirs_ref, *out_refs):
    odd = odd_ref[...] > 0
    mine_kept = ~odd if backward else odd
    which = 1 if backward else 0
    both = get_ids(send_ref)[which] == get_ids(theirs_ref)[which]
    for h in range(keep_ref.shape[0] // HEAD):
        mine, theirs = keep_ref[head(h), :].astype(F32), theirs_ref[head(h), :].astype(F32)
        state = jnp.where(both, mine + theirs, jnp.where(mine_kept, mine, theirs)).astype(BF)
        for start, ref in zip(starts, out_refs):
            if start <= h < start + ref.shape[0] // HEAD:
                ref[head(h - start), :] = state
    mine, theirs = send_ref[-2 * IDS :, :].astype(F32), theirs_ref[-2 * IDS :, :].astype(F32)
    for ref in out_refs:
        if ref.shape[0] % HEAD:
            ref[-2 * IDS :, :] = jnp.where(mine_kept, mine, theirs).astype(BF)


def edge_kernel(odd_ref, keep_ref, send_ref, theirs_ref, far_rear_ref, far_ref, near_ref, mine_ref, other_ref):
    odd = odd_ref[...] > 0
    ours, others = get_ids(send_ref), get_ids(theirs_ref)
    last_even = jnp.where(odd, others[0], ours[0])
    first_even = jnp.where(odd, others[1], ours[1])
    first_odd = jnp.where(odd, ours[1], others[1])
    take_near, take_far = get_ids(near_ref)[0] == first_even, get_ids(far_ref)[0] == first_even
    take_part = first_odd == last_even
    take_outer = take_part & (last_even == first_even)
    front = far_ref.shape[0] // HEAD
    for h in range(keep_ref.shape[0] // HEAD):
        far = far_ref[head(h), :] if h < front else far_rear_ref[head(h - front), :]
        outer = jnp.where(take_near, near_ref[head(h), :].astype(F32), 0.0)
        outer = outer + jnp.where(take_far, far.astype(F32), 0.0)
        part = jnp.where(odd, theirs_ref[head(h), :].astype(F32), keep_ref[head(h), :].astype(F32))
        joined = jnp.where(take_part, part, 0.0) + jnp.where(take_outer, outer, 0.0)
        mine_ref[head(h), :] = jnp.where(odd, joined, outer).astype(BF)
        other_ref[head(h), :] = jnp.where(odd, outer, joined).astype(BF)


def merged(odd_ref, mine_ref, other_ref):
    odd = odd_ref[...] > 0
    half = mine_ref.shape[0] // HEAD

    def state(h):
        mine, other = mine_ref[head(h % half), :].astype(F32), other_ref[head(h % half), :].astype(F32)
        return (jnp.where(odd, other, mine) if h < half else jnp.where(odd, mine, other)).astype(BF)

    return state


def local_kernel(
    ids_ref, q_hbm, k_ref, v_ref, g_hbm, c_hbm, scores_ref, local_ref, up_ref, lead_q_ref, lead_qt_ref,
    q_ref, g_ref, c_ref, sems,
):
    loads = ((q_hbm, q_ref), (g_hbm, g_ref), (c_hbm, c_ref))
    copies = [pltpu.make_async_copy(hbm, ref, sems.at[i]) for i, (hbm, ref) in enumerate(loads)]
    for copy in copies:
        copy.start()
    ids = ids_ref[...]
    length = ids.shape[1]
    at = lax.broadcasted_iota(jnp.int32, (length, length), 0)
    of = lax.broadcasted_iota(jnp.int32, (length, length), 1)
    causal = (of <= at) & (column(ids, length) == ids)
    hit = (column(ids, HEAD) == ids[:, :1]).astype(F32)
    for copy in copies:
        copy.wait()
    for h in range(q_ref.shape[1] // HEAD):
        scores = dot(q_ref[:, head(h)], k_ref[:, head(h)], NT)
        scores = jnp.where(causal, scores, 0.0).astype(BF)
        scores_ref[h] = scores
        local_ref[:, head(h)] = dot(scores, v_ref[:, head(h)], NN)
        gate = jax.nn.sigmoid(g_ref[:, head(h)].astype(F32))
        up_ref[:, head(h)] = c_ref[:, head(h)].astype(F32) * gate
        lead_q = q_ref[:, head(h)].astype(F32) * hit
        lead_q_ref[:, head(h)] = lead_q.astype(BF)
        lead_qt_ref[head(h), :] = lead_q.T.astype(BF)


def attend_kernel(odd_ref, mine_ref, other_ref, lead_q_ref, local_ref, up_ref, before_ref, attended_ref, sums_ref):
    length, states = lead_q_ref.shape
    entering = merged(odd_ref, mine_ref, other_ref)
    square = jnp.zeros((length, HEAD), F32)
    cross = jnp.zeros((length, HEAD), F32)
    for h in range(states // HEAD):
        before = entering(h)
        before_ref[head(h), :] = before
        attended = local_ref[:, head(h)] + dot(lead_q_ref[:, head(h)], before, NN)
        attended_ref[:, head(h)] = attended
        square = square + attended * attended
        cross = cross + up_ref[:, head(h)] * attended
    sums_ref[0:1, :] = jnp.sum(square.T, axis=0, keepdims=True)
    sums_ref[1:2, :] = jnp.sum(cross.T, axis=0, keepdims=True)


def scales(parts):
    total = parts[0][...]
    for part in parts[1:]:
        total = total + part[...]
    inverse = lax.rsqrt(total[0:1, :] / FEATURES + EPSILON)
    factor = inverse * inverse * inverse * total[1:2, :] / FEATURES
    return inverse, factor


def lead_kernel(ids_ref, s0, s1, s2, s3, lead_qt_ref, attended_ref, up_ref, grad_ref, out_ref):
    inverse, factor = scales((s0, s1, s2, s3))
    inverse, factor = column(inverse, HEAD), column(factor, HEAD)
    put_ids(ids_ref[...], out_ref)
    for h in range(up_ref.shape[1] // HEAD):
        grad = up_ref[:, head(h)] * inverse - attended_ref[:, head(h)] * factor
        grad = grad.astype(BF)
        grad_ref[:, head(h)] = grad
        out_ref[head(h), :] = dot(lead_qt_ref[head(h), :], grad, NN).astype(BF)


def back_kernel(
    ids_ref, s0, s1, s2, s3, q_ref, k_ref, v_ref, g_ref, scores_ref, attended_ref, up_ref, grad_ref, before_ref,
    query_grad_ref, gate_grad_ref, key_part_ref, value_part_ref, tail_k_ref, tail_v_ref,
):
    ids = ids_ref[...]
    length = ids.shape[1]
    inverse, _ = scales((s0, s1, s2, s3))
    inverse = column(inverse, HEAD)
    hit = (column(ids, HEAD) == ids[:, :1]).astype(F32).astype(BF)
    tail_hit = (column(ids, HEAD) == ids[:, -1:]).astype(F32).astype(BF)
    at = lax.broadcasted_iota(jnp.int32, (length, length), 0)
    of = lax.broadcasted_iota(jnp.int32, (length, length), 1)
    causal = (of <= at) & (column(ids, length) == ids)
    for h in range(q_ref.shape[1] // HEAD):
        grad = grad_ref[:, head(h)]
        back = jnp.where(causal, dot(grad, v_ref[:, head(h)], NT), 0.0).astype(BF)
        query_grad = dot(back, k_ref[:, head(h)], NN) + dot(grad * hit, before_ref[head(h), :], NT)
        query_grad_ref[:, head(h)] = query_grad.astype(BF)
        key_part_ref[:, head(h)] = dot(back, q_ref[:, head(h)], TN)
        value_part_ref[:, head(h)] = dot(scores_ref[h], grad, TN)
        gate = jax.nn.sigmoid(g_ref[:, head(h)].astype(F32))
        gate_grad = up_ref[:, head(h)] * attended_ref[:, head(h)] * inverse * (1.0 - gate)
        gate_grad_ref[:, head(h)] = gate_grad.astype(BF)
        tail_k_ref[:, head(h)] = k_ref[:, head(h)] * tail_hit
        tail_v_ref[:, head(h)] = v_ref[:, head(h)] * tail_hit


def finish_kernel(
    odd_ref, mine_ref, theirs_ref, front_ref, front_other_ref, rear_ref, rear_other_ref, tail_k_ref, tail_v_ref,
    key_part_ref, value_part_ref, key_grad_hbm, value_grad_hbm, key_grad_ref, value_grad_ref, key_sem, value_sem,
):
    odd = odd_ref[...] > 0
    (last, first), (their_last, their_first) = get_ids(mine_ref), get_ids(theirs_ref)
    edge = jnp.where(odd, last, their_last)
    take_came, take_other = get_ids(front_ref)[1] == edge, get_ids(front_other_ref)[1] == edge
    take_theirs = ~odd & (their_first == last)
    take_outer = odd | (take_theirs & (their_first == their_last))
    came = [(front_ref, front_other_ref, h) for h in range(front_ref.shape[0] // HEAD)]
    came += [(rear_ref, rear_other_ref, h) for h in range(rear_ref.shape[0] // HEAD)]
    copies = []

    def send(ref, hbm, sem, h):
        copies.append(pltpu.make_async_copy(ref.at[:, head(h)], hbm.at[:, head(h)], sem.at[h]))
        copies[-1].start()

    for h, (came_ref, other_ref, at) in enumerate(came):
        outer = jnp.where(take_came, came_ref[head(at), :].astype(F32), 0.0)
        outer = outer + jnp.where(take_other, other_ref[head(at), :].astype(F32), 0.0)
        after = jnp.where(take_theirs, theirs_ref[head(h), :].astype(F32), 0.0)
        after = (after + jnp.where(take_outer, outer, 0.0)).astype(BF)
        key_grad = key_part_ref[:, head(h)] + dot(tail_v_ref[:, head(h)], after, NT)
        key_grad_ref[:, head(h)] = key_grad.astype(BF)
        send(key_grad_ref, key_grad_hbm, key_sem, h)
        value_grad = value_part_ref[:, head(h)] + dot(tail_k_ref[:, head(h)], after, NN)
        value_grad_ref[:, head(h)] = value_grad.astype(BF)
        send(value_grad_ref, value_grad_hbm, value_sem, h)
    for copy in copies:
        copy.wait()


VMEM = pl.BlockSpec(memory_space=pltpu.VMEM)
HBM = pl.BlockSpec(memory_space=pltpu.HBM)


def in_hbm(x):
    return pltpu.with_memory_space_constraint(x, pltpu.HBM)


def call(kernel, outs, flops, *args, name=None, in_specs=None, out_specs=None, scratch=()):
    size = sum(math.prod(a.shape) * jnp.dtype(a.dtype).itemsize for a in (*args, *outs))
    return pl.pallas_call(
        kernel,
        out_shape=outs,
        in_specs=in_specs or [VMEM] * len(args),
        out_specs=out_specs or [VMEM] * len(outs),
        scratch_shapes=scratch,
        compiler_params=pltpu.CompilerParams(vmem_limit_bytes=24 * MIB),
        cost_estimate=pl.CostEstimate(flops=flops, bytes_accessed=size, transcendentals=0),
        name=name or kernel.__name__,
    )(*args)


def body(queries, keys, values, gates, cotangent, doc_ids):
    length, states = queries.shape
    count, ranks = lax.axis_size("ctx"), lax.axis_size("tp")
    heads = states // HEAD
    shape = jax.ShapeDtypeStruct
    ids = doc_ids.reshape(1, length)
    odd = jnp.broadcast_to(lax.rem(lax.axis_index("ctx"), 2), (1, HEAD))
    half = shape((states // 2, HEAD), BF)
    message = shape((states // 2 + 2 * IDS, HEAD), BF)
    whole = shape((states + 2 * IDS, HEAD), BF)
    wide = shape((length, states), F32)
    narrow = shape((length, states), BF)
    unit = 2 * length * length * states
    buffer, sems = pltpu.VMEM((length, states), BF), pltpu.SemaphoreType.DMA((heads,))

    def swap(x):
        return lax.ppermute(x, "ctx", [(i, i ^ 1) for i in range(count)])

    def shift(x, blocks, wrap=True):
        pairs = [(i, (i + blocks) % count) for i in range(count) if wrap or 0 <= i + blocks < count]
        return lax.ppermute(x, "ctx", pairs)

    def chip(backward, starts, outs, *parts):
        name = "chip_lead" if backward else "chip_tail"
        return call(functools.partial(chip_kernel, backward, starts), outs, 0, odd, *parts, name=name)

    ids, keys, values, tail, tail_sent = call(
        tail_kernel,
        [pltpu.VMEM(ids.shape, ids.dtype)] + [pltpu.VMEM(a.shape, a.dtype) for a in (narrow, narrow, half, message)],
        unit // 2, in_hbm(ids), in_hbm(keys), in_hbm(values), odd,
        in_specs=[HBM] * 3 + [VMEM], scratch=[pltpu.VMEM((states, length), BF), pltpu.SemaphoreType.DMA((4,))],
    )
    tail_theirs = swap(tail_sent)
    outs = [message, shape((2 * HEAD + 2 * IDS, HEAD), BF), shape(((heads // 2 - 2) * HEAD, HEAD), BF)]
    state, front, rear = chip(False, (0, 0, 2), outs, tail, tail_sent, tail_theirs)
    near, far, far_rear = shift(state, 2), shift(front, 4), shift(rear, 4, False)
    ids, _ = lax.optimization_barrier((ids, state))
    scores, local, up, lead_q, lead_qt = call(
        local_kernel, [shape((heads, length, length), BF), wide, wide, narrow, shape((states, length), BF)], 2 * unit,
        ids, in_hbm(queries), keys, values, in_hbm(gates), in_hbm(cotangent),
        in_specs=[VMEM, HBM, VMEM, VMEM, HBM, HBM], scratch=[buffer] * 3 + [pltpu.SemaphoreType.DMA((3,))],
    )
    far_rear, far, near, local = lax.optimization_barrier((far_rear, far, near, local))
    mine, given = call(edge_kernel, [half, half], 0, odd, tail, tail_sent, tail_theirs, far_rear, far, near)
    before, attended, sums = call(
        attend_kernel, [shape((states, HEAD), BF), wide, shape((2, length), F32)], unit // 2,
        odd, mine, swap(given), lead_q, local, up,
    )
    parts = [sums] + [lax.ppermute(sums, "tp", [(i, i ^ step) for i in range(ranks)]) for step in (1, 3, 2)]
    grad, lead = call(lead_kernel, [narrow, whole], unit // 2, ids, *parts, lead_qt, attended, up)

    def spread(x, wrap):
        pairs = [(i, i - (2 if i % 2 == 0 else 4)) for i in range(count)]
        useful = [(i, j) for i, j in pairs if j >= 0]
        spare = [(0, count - 3), (1, count - 2), (3, count - 1)] if wrap else []
        return lax.ppermute(x, "ctx", useful + spare)

    lead_theirs = swap(lead)
    cut = 6 * heads // 8
    outs = [shape((cut * HEAD + 2 * IDS, HEAD), BF), shape(((heads - cut) * HEAD, HEAD), BF)]
    front, rear = chip(True, (0, cut), outs, lead, lead, lead_theirs)
    front_came, rear_came = spread(front, True), spread(rear, False)
    ids, _ = lax.optimization_barrier((ids, front))
    query_grad, gate_grad, key_part, value_part, tail_k, tail_v = call(
        back_kernel, [narrow, narrow, wide, wide, narrow, narrow], 5 * unit,
        ids, *parts, queries, keys, values, gates, scores, attended, up, grad, before,
    )
    rear_came, front_came, key_part = lax.optimization_barrier((rear_came, front_came, key_part))
    key_grad, value_grad = call(
        finish_kernel, [narrow, narrow], unit, odd, lead, lead_theirs, front_came, swap(front_came), rear_came,
        swap(rear_came), tail_k, tail_v, key_part, value_part, out_specs=[HBM] * 2, scratch=[buffer, buffer, sems, sems],
    )
    return query_grad, key_grad, value_grad, gate_grad


def solution(mesh):
    return jax.shard_map(
        body,
        mesh=mesh,
        in_specs=(P("ctx", "tp"),) * 5 + (P("ctx"),),
        out_specs=(P("ctx", "tp"),) * 4,
        check_vma=False,
    )
```
